32 devices in a mesh: expert: 2 (over x), replica: 16 (over z, y, core).
Axes of the slice: x: 2, y: 2, z: 4, core: 2. Of those that a mesh axis runs over, the one named last changes fastest.
Arguments:
- pool: bfloat16 [16, 4096, 2048], P('replica', 'expert'), may hold values from -15 to 15
- row_index: int32 [2, 16, 256], P(None, 'replica'), may hold values from 0 to 4095, as said below
- counts: int32 [2, 16], P('expert', 'replica'), may hold values from 128 to 256, as said below
- targets: bfloat16 [2, 16, 256, 384], P('expert', 'replica'), may hold values from -4 to 4
- weights: float32 [2, 2, 2048, 384], P('expert', None, 'replica'), may hold values from -0.125 to 0.125
- first_moment: float32 [2, 2, 2048, 384], P('expert', None, 'replica'), may hold values from -1.5 to 1.5
- second_moment: float32 [2, 2, 2048, 384], P('expert', None, 'replica'), may hold values from 0.0001 to 0.01
Outputs:
- new_weights: float32 [2, 2, 2048, 384], P('expert', None, 'replica')
- new_first_moment: float32 [2, 2, 2048, 384], P('expert', None, 'replica')
- new_second_moment: float32 [2, 2, 2048, 384], P('expert', None, 'replica')
The draws below stay inside these ranges and needn't reach their ends.
Inputs may be any that keep to these rules, and one draw needn't show every extreme that they name: `row_index`: for each expert and replica the 256 entries are distinct rows of that replica's 4096 tokens; at most 192 of them lie in any one aligned block of 2048 rows, and some block holds exactly 192 of them. `counts`: at least 128 live slots for each expert on each replica; some expert on some replica has all 256 slots live.
All inputs are finite; a program needn't handle non-finite values.
Results may differ from the reference program's by a relative error of at most 0.0043.
Values may be sent and summed in bfloat16 or wider, within the bound.
No kernel may reach another device: no remote copies, remote signals or barrier semaphores. Data moves between devices by JAX's collectives and lax.ppermute only.
A program may use at most 64 MiB of HBM per device.

```python
import math
import jax
import jax.numpy as jnp
from jax import lax

D = 2048
F = 384
TOKENS = 4096
STEP = 3
CAP = 256
EXPERTS = 2
REPLICAS = 16
SHARD_MOST = 192
LEVELS = 4


def draw_pool(key, part):
    block_rows = D // REPLICAS
    place = (jnp.arange(REPLICAS, dtype=jnp.float32) + jax.random.uniform(jax.random.fold_in(key, 41), (REPLICAS,), jnp.float32)) / REPLICAS
    block_mean = 2.0 * place
    column_scale = jnp.exp(jax.random.uniform(jax.random.fold_in(key, 43), (D,), jnp.float32, math.log(0.3), math.log(3.0)))
    noise = jax.random.truncated_normal(jax.random.fold_in(key, 44), -4.0, 4.0, (REPLICAS, TOKENS, D), jnp.float32)
    even_column = (jnp.arange(D, dtype=jnp.int32) % 2 == 0).astype(jnp.float32)
    column_mean = jnp.repeat(block_mean, block_rows) * even_column
    return (column_mean[None, None, :] + column_scale[None, None, :] * noise).astype(jnp.bfloat16)


def draw_row_index(key, part):
    shard_rows = TOKENS // EXPERTS
    base_share = CAP // EXPERTS
    extra_share = SHARD_MOST - base_share
    list_count = EXPERTS * REPLICAS
    pair_count = EXPERTS // 2
    shift_draw = jax.random.randint(jax.random.fold_in(key, 31), (list_count, pair_count), 0, extra_share + 1)
    forced_pair = jax.random.randint(jax.random.fold_in(key, 32), (list_count,), 0, pair_count)
    shifts = jnp.where(jnp.arange(pair_count, dtype=jnp.int32)[None, :] == forced_pair[:, None], extra_share, shift_draw)
    paired = jnp.stack([base_share + shifts, base_share - shifts], axis=2).reshape(list_count, EXPERTS)
    order_keys = jax.random.split(jax.random.fold_in(key, 33), list_count)
    shard_order = jax.vmap(lambda sub_key: jax.random.permutation(sub_key, EXPERTS))(order_keys)
    per_shard = jnp.take_along_axis(paired, shard_order, axis=1)
    row_keys = jax.random.split(jax.random.fold_in(key, 34), list_count * EXPERTS)
    picks = jax.vmap(lambda sub_key: jax.random.permutation(sub_key, shard_rows)[:SHARD_MOST])(row_keys)
    picks = picks.reshape(list_count, EXPERTS, SHARD_MOST)
    rows = picks + (jnp.arange(EXPERTS, dtype=jnp.int32) * shard_rows)[None, :, None]
    valid = (jnp.arange(SHARD_MOST, dtype=jnp.int32)[None, None, :] < per_shard[:, :, None]).astype(jnp.int32)
    total_candidates = EXPERTS * SHARD_MOST
    scores = (1 - valid.reshape(list_count, total_candidates)) * total_candidates + jnp.arange(total_candidates, dtype=jnp.int32)[None, :]
    chosen_order = jnp.argsort(scores, axis=1)[:, :CAP]
    chosen = jnp.take_along_axis(rows.reshape(list_count, total_candidates), chosen_order, axis=1)
    slot_keys = jax.random.split(jax.random.fold_in(key, 35), list_count)
    slot_order = jax.vmap(lambda sub_key: jax.random.permutation(sub_key, CAP))(slot_keys)
    result = jnp.take_along_axis(chosen, slot_order, axis=1)
    return result.reshape(EXPERTS, REPLICAS, CAP).astype(jnp.int32)


def draw_counts(key, part):
    drawn_counts = jax.random.randint(jax.random.fold_in(key, 21), (EXPERTS * REPLICAS,), CAP // 2, CAP + 1)
    full_place = jax.random.randint(jax.random.fold_in(key, 22), (), 0, EXPERTS * REPLICAS)
    places = jnp.arange(EXPERTS * REPLICAS, dtype=jnp.int32)
    filled = jnp.where(places == full_place, CAP, drawn_counts)
    return filled.reshape(EXPERTS, REPLICAS).astype(jnp.int32)


def draw_targets(key, part):
    signs = (2 * jax.random.randint(jax.random.fold_in(key, 51), (EXPERTS, 1, 1, F), 0, 2) - 1).astype(jnp.float32)
    level = jax.random.uniform(jax.random.fold_in(key, 52), (EXPERTS, 1, 1, F), jnp.float32, 0.5, 1.5)
    noise = 0.5 * jax.random.truncated_normal(jax.random.fold_in(key, 53), -4.0, 4.0, (EXPERTS, REPLICAS, CAP, F), jnp.float32)
    return (signs * level + noise).astype(jnp.bfloat16)


def block_levels(key, extent, cuts, smallest, largest):
    def one(dim, blocks):
        steps = jax.random.uniform(jax.random.fold_in(jax.random.fold_in(key, 6), dim), (blocks,), jnp.float32, smallest / len(cuts), largest / len(cuts))
        return jnp.repeat(jnp.exp(steps), extent[dim] // blocks).reshape((-1,) + (1,) * (len(extent) - dim - 1))

    factor_of = one(*cuts[0])
    for cut in cuts[1:]:
        factor_of = factor_of * one(*cut)
    return factor_of


def gaussian(stream_key, extent, scale, reach, cuts=(), held_as=jnp.bfloat16):
    values = jax.random.normal(stream_key, extent, jnp.float32) * scale
    if len(cuts) > 0:
        values = block_levels(stream_key, extent, cuts, -0.22, 0.18) * values
    return jnp.clip(values, min=-reach, max=reach).astype(held_as)


def setup_inputs(seed: int = 0) -> dict:
    key_of = jax.random.split(jax.random.key(seed), 8)
    pool = draw_pool(jax.random.fold_in(key_of[7], 71), 0)
    row_index = draw_row_index(jax.random.fold_in(key_of[7], 71), 0)
    counts = draw_counts(jax.random.fold_in(key_of[7], 71), 0)
    targets = draw_targets(jax.random.fold_in(key_of[7], 71), 0)
    weights = gaussian(key_of[4], (EXPERTS, 2, D, F), D ** -0.5, 0.125, ((0, 2), (2, 16)), jnp.float32)
    first_moment = gaussian(key_of[5], (EXPERTS, 2, D, F), 0.1, 1.5, ((0, 2), (2, 16)), jnp.float32)
    second_moment = jnp.clip(jnp.exp(math.log(0.01) - 4.6051702 * jax.random.uniform(key_of[6], (EXPERTS, 2, D, F), jnp.float32) ** block_levels(key_of[6], (EXPERTS, 2, D, F), ((0, 2), (2, 16)), -0.2, 0.2)), 0.0001, 0.01)
    return dict(pool=pool, row_index=row_index, counts=counts, targets=targets, weights=weights, first_moment=first_moment, second_moment=second_moment)


beta_first = 0.9
beta_second = 0.999
learning_rate = 0.02
decay_rate = 0.1
adam_epsilon = 1e-08
adasum_epsilon = 1e-12

def replica_gradient(pool_rows, selected, live_count, target_rows, gate_matrix, up_matrix):
    inputs = pool_rows[selected.astype(jnp.int32)]
    gate_value = jnp.dot(inputs, gate_matrix, preferred_element_type=jnp.float32)
    up_value = jnp.dot(inputs, up_matrix, preferred_element_type=jnp.float32)
    sigmoid = jax.nn.sigmoid(gate_value)
    activated = gate_value * sigmoid
    silu_slope = sigmoid * (1.0 + gate_value * (1.0 - sigmoid))
    live = (lax.iota(jnp.int32, selected.shape[0]) < live_count).astype(jnp.float32)[:, None]
    residual = (activated * up_value - target_rows.astype(jnp.float32)) * live / live_count.astype(jnp.float32)
    gate_delta = (residual * up_value * silu_slope).astype(jnp.bfloat16)
    up_delta = (residual * activated).astype(jnp.bfloat16)
    gate_grad = jnp.dot(inputs.T, gate_delta, preferred_element_type=jnp.float32)
    up_grad = jnp.dot(inputs.T, up_delta, preferred_element_type=jnp.float32)
    return jnp.stack([gate_grad, up_grad])

def adasum_tree(gradients):
    for level_number in range(LEVELS):
        half_count = gradients.shape[0] // 2
        first_group = gradients[:half_count]
        second_group = gradients[half_count:]
        inner_product = lax.optimization_barrier(jnp.sum(first_group * second_group, axis=(2, 3), keepdims=True))
        first_square = lax.optimization_barrier(jnp.sum(first_group * first_group, axis=(2, 3), keepdims=True))
        second_square = lax.optimization_barrier(jnp.sum(second_group * second_group, axis=(2, 3), keepdims=True))
        first_weight = 1.0 - inner_product / (2.0 * first_square + adasum_epsilon)
        second_weight = 1.0 - inner_product / (2.0 * second_square + adasum_epsilon)
        gradients = first_weight * first_group + second_weight * second_group
    return gradients[0]

def adam_update(gradient, weight, moment_one, moment_two):
    moment_one = beta_first * moment_one + (1.0 - beta_first) * gradient
    moment_two = beta_second * moment_two + (1.0 - beta_second) * gradient * gradient
    first_hat = moment_one / (1.0 - beta_first ** STEP)
    second_hat = moment_two / (1.0 - beta_second ** STEP)
    weight = weight - learning_rate * (first_hat / (jnp.sqrt(second_hat) + adam_epsilon) + decay_rate * weight)
    return (weight, moment_one, moment_two)

def reference(pool, row_index, counts, targets, weights, first_moment, second_moment):
    lowered = weights.astype(jnp.bfloat16)

    def one_expert(expert_args):
        expert_rows, expert_counts, expert_targets, expert_lowered, expert_weight, moment_one, moment_two = expert_args

        def one_replica(replica_args):
            pool_rows, selected, live_count, target_rows = replica_args
            return replica_gradient(pool_rows, selected, live_count, target_rows, expert_lowered[0], expert_lowered[1])
        gradients = lax.map(one_replica, (pool, expert_rows, expert_counts, expert_targets))
        combined = adasum_tree(gradients)
        return adam_update(combined, expert_weight, moment_one, moment_two)
    return lax.map(one_expert, (row_index, counts, targets, lowered, weights, first_moment, second_moment))
```

```python
import functools

import jax
import jax.numpy as jnp
from jax import lax
from jax.experimental import pallas as pl
from jax.experimental.pallas import tpu as pltpu
from jax.sharding import PartitionSpec as P

STEP = 3


beta_first = 0.9
beta_second = 0.999
learning_rate = 0.02
decay_rate = 0.1
adam_epsilon = 1e-08
adasum_epsilon = 1e-12

CORE, SIDE = 1, 2
VMEM_LIMIT = 50 * 1024 * 1024
f32, bf16, i32 = jnp.float32, jnp.bfloat16, jnp.int32


def swapped(x, axis, mask):
    return lax.ppermute(x, axis, [(i, i ^ mask) for i in range(lax.axis_size(axis))])


def vmem():
    return pl.BlockSpec(memory_space=pltpu.VMEM)


def smem():
    return pl.BlockSpec(memory_space=pltpu.SMEM)


def params():
    return pltpu.CompilerParams(vmem_limit_bytes=VMEM_LIMIT)


def adam_update(gradient, weight, moment_one, moment_two):
    moment_one = beta_first * moment_one + (1.0 - beta_first) * gradient
    moment_two = beta_second * moment_two + (1.0 - beta_second) * gradient * gradient
    first_hat = moment_one / (1.0 - beta_first**STEP)
    second_hat = moment_two / (1.0 - beta_second**STEP)
    weight = weight - learning_rate * (
        first_hat / (jnp.sqrt(second_hat) + adam_epsilon) + decay_rate * weight
    )
    return (weight, moment_one, moment_two)


def grid_iota(shape, dim):
    return lax.broadcasted_iota(i32, shape, dim)


def compacted_rows(listed, block, shard_rows, most):
    slots = listed.shape[1]
    local = listed - block * shard_rows
    held = (local >= 0) & (local < shard_rows)
    down, along = grid_iota((slots, slots), 0), grid_iota((slots, slots), 1)
    held_wide = jnp.broadcast_to(held.astype(i32), (slots, slots))
    held_column = jnp.sum(jnp.where(down == along, held_wide, 0), axis=1, keepdims=True)
    rank = jnp.sum(jnp.where(down < along, jnp.broadcast_to(held_column, (slots, slots)), 0), axis=0, keepdims=True)
    place = jnp.where(held, rank, -1)
    hit = grid_iota((most, slots), 0) == jnp.broadcast_to(place, (most, slots))
    return jnp.sum(jnp.where(hit, jnp.broadcast_to(local + 1, (most, slots)), 0), axis=1, keepdims=True) - 1


def slot_rows(listed, block, shard_rows):
    slots = listed.shape[1]
    local = listed - block * shard_rows
    held = (local >= 0) & (local < shard_rows)
    value = jnp.where(held, local + 1, 0)
    diagonal = grid_iota((slots, slots), 0) == grid_iota((slots, slots), 1)
    return jnp.sum(jnp.where(diagonal, jnp.broadcast_to(value, (slots, slots)), 0), axis=1, keepdims=True) - 1


def slot_ranks(listed, block, shard_rows):
    slots = listed.shape[1]
    local = listed - block * shard_rows
    held = ((local >= 0) & (local < shard_rows)).astype(i32)
    held_wide = jnp.broadcast_to(held, (slots, slots))
    down, along = grid_iota((slots, slots), 0), grid_iota((slots, slots), 1)
    rank = jnp.sum(jnp.where(along < down, held_wide, 0), axis=1, keepdims=True)
    own = jnp.sum(jnp.where(along == down, held_wide, 0), axis=1, keepdims=True)
    return jnp.where(own > 0, rank, -1)


def one_hot(column, width):
    return (grid_iota((column.shape[0], width), 1) == column).astype(f32).astype(bf16)


def outgoing_kernel(experts, most, where_ref, index_ref, pool_ref, out_ref, pick_ref):
    shard_rows = pool_ref.shape[0]
    me = where_ref[0]

    @pl.when(pl.program_id(0) == 0)
    def _():
        for mask in range(1, experts):
            listed = index_ref[pl.ds(me ^ mask, 1), :]
            pick_ref[mask - 1] = one_hot(compacted_rows(listed, me, shard_rows, most), shard_rows)

    for mask in range(1, experts):
        out_ref[mask - 1] = jnp.dot(pick_ref[mask - 1], pool_ref[...], preferred_element_type=f32).astype(bf16)


def outgoing_rows(where, index, pool, experts, most, part):
    shard_rows, width = pool.shape
    steps = 2
    chunk = width // (2 * steps)
    return pl.pallas_call(
        functools.partial(outgoing_kernel, experts, most),
        out_shape=jax.ShapeDtypeStruct((experts - 1, most, width // 2), bf16),
        grid_spec=pltpu.PrefetchScalarGridSpec(
            num_scalar_prefetch=1,
            grid=(steps,),
            in_specs=[
                pl.BlockSpec(index.shape, lambda i, w: (0, 0)),
                pl.BlockSpec((shard_rows, chunk), lambda i, w: (0, (w[1] ^ 1 ^ part) * steps + i)),
            ],
            out_specs=pl.BlockSpec((experts - 1, most, chunk), lambda i, w: (0, 0, i)),
            scratch_shapes=[pltpu.VMEM((experts - 1, most, shard_rows), bf16)],
        ),
        compiler_params=params(),
        name="outgoing_rows",
    )(where, index, pool)


def own_kernel(where_ref, index_ref, pool_ref, out_ref, pick_ref):
    me = where_ref[0]

    @pl.when(pl.program_id(0) == 0)
    def _():
        listed = index_ref[pl.ds(me, 1), :]
        pick_ref[...] = one_hot(slot_rows(listed, me, pool_ref.shape[0]), pool_ref.shape[0])

    out_ref[0] = jnp.dot(pick_ref[...], pool_ref[...], preferred_element_type=f32).astype(bf16)


def own_rows(where, index, pool):
    shard_rows, width = pool.shape
    slots = index.shape[1]
    steps = 2
    chunk = width // (2 * steps)
    return pl.pallas_call(
        own_kernel,
        out_shape=jax.ShapeDtypeStruct((2, slots, width // 2), bf16),
        grid_spec=pltpu.PrefetchScalarGridSpec(
            num_scalar_prefetch=1,
            grid=(2 * steps,),
            in_specs=[
                pl.BlockSpec(index.shape, lambda i, w: (0, 0)),
                pl.BlockSpec((shard_rows, chunk), lambda i, w: (0, (w[1] ^ 1 ^ (i // steps)) * steps + i % steps)),
            ],
            out_specs=pl.BlockSpec((1, slots, chunk), lambda i, w: (i // steps, 0, i % steps)),
            scratch_shapes=[pltpu.VMEM((slots, shard_rows), bf16)],
        ),
        compiler_params=params(),
        name="own_rows",
    )(where, index, pool)


def merge_kernel(experts, part, uppers, shard_rows, where_ref, index_ref, own_ref, *refs):
    incoming, outs = refs[: experts - 1], refs[experts - 1 :]
    me, upper, core = where_ref[0], where_ref[2], where_ref[3]
    most = incoming[0].shape[1]
    quarter = own_ref.shape[2] // (uppers // 2)
    block = quarter // 4
    listed = index_ref[pl.ds(me, 1), :]
    picks = [one_hot(slot_ranks(listed, me ^ mask, shard_rows), most) for mask in range(1, experts)]
    for position in range(uppers // 2):
        mask = position + (uppers // 2 if part == 0 else 0)
        first = pl.multiple_of(((upper ^ mask) & (uppers // 2 - 1)) * quarter, quarter)
        columns = pl.ds(first, quarter)
        rows = own_ref[0, :, columns].astype(f32)
        for pick, ref in zip(picks, incoming):
            rows = rows + jnp.dot(pick, ref[0, :, columns], preferred_element_type=f32)
        rows = rows.astype(bf16)
        for side in range(2):
            low = rows[:, 2 * side * block : (2 * side + 1) * block]
            high = rows[:, (2 * side + 1) * block : (2 * side + 2) * block]
            outs[2 * position][side] = jnp.where(core == 0, low, high)
            outs[2 * position + 1][side] = jnp.where(core == 0, high, low)


def merged_rows(where, index, own, incoming, experts, part, uppers, shard_rows):
    slots, half = own.shape[1:]
    block = half // (uppers // 2) // 4
    piece = jax.ShapeDtypeStruct((2, slots, block), bf16)
    outs = pl.pallas_call(
        functools.partial(merge_kernel, experts, part, uppers, shard_rows),
        out_shape=[piece] * uppers,
        grid=(1,),
        in_specs=[smem(), vmem(), pl.BlockSpec((1, slots, half), lambda i: (part, 0, 0))] + [vmem()] * (experts - 1),
        out_specs=[vmem()] * uppers,
        compiler_params=params(),
        name="merged_rows",
    )(where, index, own, *incoming)
    return outs[0::2], outs[1::2]


def forward_kernel(uppers, where_ref, count_ref, targets_ref, *refs):
    rows = refs[: 2 * uppers]
    blocks = refs[2 * uppers : 6 * uppers]
    kept_ref, sent_ref = refs[6 * uppers :]
    side = where_ref[4]
    slots, hidden = targets_ref.shape
    gate_value = jnp.zeros((slots, hidden), f32)
    up_value = jnp.zeros((slots, hidden), f32)
    for mask in range(uppers):
        for side_mask in range(2):
            for core_mask in range(2):
                x = rows[2 * mask + core_mask][side ^ side_mask]
                w = blocks[4 * mask + 2 * side_mask + core_mask]
                gate_value += jnp.dot(x, w[0], preferred_element_type=f32)
                up_value += jnp.dot(x, w[1], preferred_element_type=f32)
    live_count = count_ref[0, 0]
    sigmoid = jax.nn.sigmoid(gate_value)
    activated = gate_value * sigmoid
    silu_slope = sigmoid * (1.0 + gate_value * (1.0 - sigmoid))
    live = (grid_iota((slots, 1), 0) < live_count).astype(f32)
    residual = (activated * up_value - targets_ref[...].astype(f32)) * live / jnp.full((1, 1), live_count, i32).astype(f32)
    gate_delta = (residual * up_value * silu_slope).astype(bf16)
    up_delta = (residual * activated).astype(bf16)
    kept_ref[...] = jnp.where(side == 0, gate_delta, up_delta)
    sent_ref[...] = jnp.where(side == 0, up_delta, gate_delta)


def forward(where, count, targets, rows, blocks, uppers):
    out = jax.ShapeDtypeStruct(targets.shape, bf16)
    return pl.pallas_call(
        functools.partial(forward_kernel, uppers),
        out_shape=[out, out],
        in_specs=[smem(), smem()] + [vmem()] * (1 + 6 * uppers),
        out_specs=[vmem()] * 2,
        compiler_params=params(),
        name="forward_deltas",
    )(where, count, targets, *rows, *blocks)


def token_contract(left, right):
    return lax.dot_general(left, right, (((0,), (0,)), ((), ())), preferred_element_type=f32)


def gram_kernel(replicas, where_ref, *refs):
    rows, deltas = refs[:replicas], refs[replicas : 2 * replicas]
    gradient_ref, gram_ref, total_ref = refs[2 * replicas :]
    me = where_ref[5]
    block = rows[0].shape[2]
    for mask in range(replicas):
        for side in range(2):
            gradient_ref[me ^ mask, side * block : (side + 1) * block, :] = token_contract(
                rows[mask][side], deltas[mask][...]
            )
    group = 4
    depth, hidden = gradient_ref.shape[1:]
    lanes = 128
    total_ref[...] = jnp.zeros_like(total_ref)

    def pair(first, second):
        def step(k, sums):
            here = pl.ds(pl.multiple_of(8 * k, 8), 8)
            a = [gradient_ref[first * group + i, here, :] for i in range(group)]
            b = [gradient_ref[second * group + j, here, :] for j in range(group)]
            new = []
            for i in range(group):
                for j in range(group):
                    product = a[i] * b[j]
                    term = sums[i * group + j]
                    for lane in range(0, hidden, lanes):
                        term = term + product[:, lane : lane + lanes]
                    new.append(term)
            return tuple(new)

        sums = lax.fori_loop(0, depth // 8, step, tuple(jnp.zeros((8, lanes), f32) for _ in range(group * group)))
        for i in range(group):
            for j in range(group):
                total_ref[first * group + i, second * group + j] = sums[i * group + j]

    def outer(first, carry):
        def inner(second, carry):
            pair(first, second)
            return carry

        return lax.fori_loop(first, replicas // group, inner, carry)

    lax.fori_loop(0, replicas // group, outer, 0)
    reduced = jnp.sum(jnp.sum(total_ref[...], axis=2), axis=2)
    gram_ref[...] = reduced


def gram(where, rows, deltas, replicas):
    depth = 2 * rows[0].shape[2]
    hidden = deltas[0].shape[1]
    return pl.pallas_call(
        functools.partial(gram_kernel, replicas),
        out_shape=[
            jax.ShapeDtypeStruct((replicas, depth, hidden), f32),
            jax.ShapeDtypeStruct((replicas, replicas), f32),
        ],
        in_specs=[smem()] + [vmem()] * (2 * replicas),
        out_specs=[vmem()] * 2,
        scratch_shapes=[pltpu.VMEM((replicas, replicas, 8, 128), f32)],
        compiler_params=params(),
        name="gradients_and_products",
    )(where, *rows, *deltas)


def tree_weights(products, replicas, group):
    down, along = grid_iota((replicas, replicas), 0), grid_iota((replicas, replicas), 1)
    upper = jnp.where(down <= along, products, 0.0)
    table = upper + jnp.where(down < along, products, 0.0).T
    weights = jnp.ones((replicas, 1), f32)
    half = replicas // 2
    while half >= 1:
        same = down == along
        other = ((down + half) & (replicas - 1)) == along
        partner = ((along + half) & (replicas - 1)) == down
        square_down = jnp.sum(jnp.where(same, table, 0.0), axis=1, keepdims=True)
        square_along = jnp.sum(jnp.where(same, table, 0.0), axis=0, keepdims=True)
        inner_down = jnp.sum(jnp.where(other, table, 0.0), axis=1, keepdims=True)
        inner_along = jnp.sum(jnp.where(partner, table, 0.0), axis=0, keepdims=True)
        weight_down = 1.0 - inner_down / (2.0 * square_down + adasum_epsilon)
        weight_along = 1.0 - inner_along / (2.0 * square_along + adasum_epsilon)
        weights = weights * weight_down
        table = weight_down * (table * weight_along)
        table = table + jnp.concatenate([table[half:], table[:half]], axis=0)
        table = table + jnp.concatenate([table[:, half:], table[:, :half]], axis=1)
        half //= 2
    return weights


def combine_kernel(replicas, where_ref, gram_ref, gradient_ref, kept_ref, sent_ref):
    side = where_ref[4]
    block = kept_ref.shape[0]
    weights = tree_weights(gram_ref[...], replicas, 4)
    for ref, first in ((kept_ref, side), (sent_ref, 1 - side)):
        here = pl.ds(pl.multiple_of(first * block, block), block)
        total = jnp.zeros(ref.shape, f32)
        for r in range(replicas):
            total = total + weights[r : r + 1] * gradient_ref[r, here, :]
        ref[...] = total


def combine(where, products, gradients):
    replicas, depth, hidden = gradients.shape
    out = jax.ShapeDtypeStruct((depth // 2, hidden), f32)
    return pl.pallas_call(
        functools.partial(combine_kernel, replicas),
        out_shape=[out, out],
        in_specs=[smem(), vmem(), vmem()],
        out_specs=[vmem()] * 2,
        compiler_params=params(),
        name="combined_gradient",
    )(where, products, gradients)


def shards(pool, row_index, counts, targets, weights, first_moment, second_moment):
    replicas = lax.axis_size("replica")
    experts = lax.axis_size("expert")
    uppers = replicas // 4
    position = lax.axis_index("replica")
    expert_position = lax.axis_index("expert")
    core, side, upper = position & 1, position >> 1 & 1, position >> 2
    where = jnp.stack([expert_position, position // (replicas // 2), upper, core, side, position]).astype(i32)
    index = row_index[:, 0, :]
    local_pool = pool[0]
    shard_rows = local_pool.shape[0]
    most = 3 * index.shape[1] // (2 * experts)

    lowered = weights[0].astype(bf16)
    by_upper = [lowered] + [swapped(lowered, "replica", 4 * mask) for mask in range(1, uppers)]
    by_side = [[piece, swapped(piece, "replica", SIDE)] for piece in by_upper]
    blocks = []
    for pieces in by_side:
        for piece in pieces:
            blocks += [piece, swapped(piece, "replica", CORE)]

    incoming = []
    for part in range(2):
        outgoing = outgoing_rows(where, index, local_pool, experts, most, part)
        incoming.append(
            [swapped(outgoing[mask - 1 : mask], "expert", mask) for mask in range(1, experts)]
        )
    own = own_rows(where, index, local_pool)
    kept, sent = [None] * uppers, [None] * uppers
    for part in range(2):
        first = uppers // 2 if part == 0 else 0
        kept[first : first + uppers // 2], sent[first : first + uppers // 2] = merged_rows(
            where, index, own, incoming[part], experts, part, uppers, shard_rows
        )
    rows_here = [piece for pair in zip(kept, sent) for piece in pair]
    rows = [None] * replicas
    order = list(range(uppers // 2, uppers)) + list(range(uppers // 2))
    for mask in order:
        pair = [kept[mask], swapped(sent[mask], "replica", CORE)]
        for core_mask in range(2):
            piece = pair[core_mask]
            if mask > 0:
                piece = swapped(piece, "replica", 4 * mask)
            rows[4 * mask + core_mask] = piece
            rows[4 * mask + 2 + core_mask] = swapped(piece, "replica", SIDE)

    kept_delta, sent_delta = forward(where, counts, targets[0, 0], rows_here, blocks, uppers)
    side_deltas = [kept_delta, swapped(sent_delta, "replica", SIDE)]
    deltas = [None] * replicas
    for mask in order:
        for side_mask in range(2):
            piece = side_deltas[side_mask]
            if mask > 0:
                piece = swapped(piece, "replica", 4 * mask)
            deltas[4 * mask + 2 * side_mask] = piece
            deltas[4 * mask + 2 * side_mask + 1] = swapped(piece, "replica", CORE)

    gradients, products = gram(where, rows, deltas, replicas)
    products = products + swapped(products, "replica", CORE)
    mask = 4
    while mask < replicas:
        products = products + swapped(products, "replica", mask)
        mask *= 2
    kept_block, sent_block = combine(where, products, gradients)
    other_block = swapped(sent_block, "replica", SIDE)
    combined = jnp.where(
        side == 0, jnp.stack([kept_block, other_block]), jnp.stack([other_block, kept_block])
    )
    new_weight, moment_one, moment_two = adam_update(
        combined, weights[0], first_moment[0], second_moment[0]
    )
    return (new_weight[None], moment_one[None], moment_two[None])


def solution(mesh):
    in_specs = (
        P("replica", "expert", None),
        P(None, "replica", None),
        P("expert", "replica"),
        P("expert", "replica", None, None),
        P("expert", None, "replica", None),
        P("expert", None, "replica", None),
        P("expert", None, "replica", None),
    )
    out_specs = (
        P("expert", None, "replica", None),
        P("expert", None, "replica", None),
        P("expert", None, "replica", None),
    )
    return jax.shard_map(shards, mesh=mesh, in_specs=in_specs, out_specs=out_specs, check_vma=False)
```

```python
import functools

import jax
import jax.numpy as jnp
from jax import lax
from jax.experimental import pallas as pl
from jax.experimental.pallas import tpu as pltpu
from jax.sharding import PartitionSpec as P

STEP = 3


beta_first = 0.9
beta_second = 0.999
learning_rate = 0.02
decay_rate = 0.1
adam_epsilon = 1e-08
adasum_epsilon = 1e-12

CORE, SIDE = 1, 2
VMEM_LIMIT = 50 * 1024 * 1024
LIGHT = pl.CostEstimate(flops=1, bytes_accessed=1, transcendentals=0)
f32, bf16, i32 = jnp.float32, jnp.bfloat16, jnp.int32


def gathered(x, masks):
    pieces = {0: x}
    for mask in reversed(masks):
        pieces.update({mask | held: swapped(piece, "replica", mask) for held, piece in list(pieces.items())})
    return pieces


def swapped(x, axis, mask):
    return lax.ppermute(x, axis, [(i, i ^ mask) for i in range(lax.axis_size(axis))])


def vmem():
    return pl.BlockSpec(memory_space=pltpu.VMEM)


def smem():
    return pl.BlockSpec(memory_space=pltpu.SMEM)


def params():
    return pltpu.CompilerParams(vmem_limit_bytes=VMEM_LIMIT)


def adam_update(gradient, weight, moment_one, moment_two):
    moment_one = beta_first * moment_one + (1.0 - beta_first) * gradient
    moment_two = beta_second * moment_two + (1.0 - beta_second) * gradient * gradient
    first_hat = moment_one / (1.0 - beta_first**STEP)
    second_hat = moment_two / (1.0 - beta_second**STEP)
    weight = weight - learning_rate * (
        first_hat / (jnp.sqrt(second_hat) + adam_epsilon) + decay_rate * weight
    )
    return (weight, moment_one, moment_two)


def grid_iota(shape, dim):
    return lax.broadcasted_iota(i32, shape, dim)


def compacted_rows(listed, block, shard_rows, most):
    slots = listed.shape[1]
    local = listed - block * shard_rows
    held = (local >= 0) & (local < shard_rows)
    down, along = grid_iota((slots, slots), 0), grid_iota((slots, slots), 1)
    held_wide = jnp.broadcast_to(held.astype(i32), (slots, slots))
    held_column = jnp.sum(jnp.where(down == along, held_wide, 0), axis=1, keepdims=True)
    rank = jnp.sum(jnp.where(down < along, jnp.broadcast_to(held_column, (slots, slots)), 0), axis=0, keepdims=True)
    place = jnp.where(held, rank, -1)
    hit = grid_iota((most, slots), 0) == jnp.broadcast_to(place, (most, slots))
    return jnp.sum(jnp.where(hit, jnp.broadcast_to(local + 1, (most, slots)), 0), axis=1, keepdims=True) - 1


def slot_rows(listed, block, shard_rows):
    slots = listed.shape[1]
    local = listed - block * shard_rows
    held = (local >= 0) & (local < shard_rows)
    value = jnp.where(held, local + 1, 0)
    diagonal = grid_iota((slots, slots), 0) == grid_iota((slots, slots), 1)
    return jnp.sum(jnp.where(diagonal, jnp.broadcast_to(value, (slots, slots)), 0), axis=1, keepdims=True) - 1


def slot_ranks(listed, block, shard_rows):
    slots = listed.shape[1]
    local = listed - block * shard_rows
    held = ((local >= 0) & (local < shard_rows)).astype(i32)
    held_wide = jnp.broadcast_to(held, (slots, slots))
    down, along = grid_iota((slots, slots), 0), grid_iota((slots, slots), 1)
    rank = jnp.sum(jnp.where(along < down, held_wide, 0), axis=1, keepdims=True)
    own = jnp.sum(jnp.where(along == down, held_wide, 0), axis=1, keepdims=True)
    return jnp.where(own > 0, rank, -1)


def one_hot(column, width):
    return (grid_iota((column.shape[0], width), 1) == column).astype(f32).astype(bf16)


def listed_kernel(experts, most, where_ref, index_ref, pool_ref, out_ref, own_ref, pick_ref):
    shard_rows = pool_ref.shape[0]
    slots = index_ref.shape[1]
    me = where_ref[0]

    @pl.when(pl.program_id(0) == 0)
    def _():
        pick_ref[:slots] = one_hot(slot_rows(index_ref[pl.ds(me, 1), :], me, shard_rows), shard_rows)
        for mask in range(1, experts):
            listed = index_ref[pl.ds(me ^ mask, 1), :]
            first = slots + (mask - 1) * most
            pick_ref[first : first + most] = one_hot(compacted_rows(listed, me, shard_rows, most), shard_rows)

    rows = jnp.dot(pick_ref[...], pool_ref[...], preferred_element_type=f32).astype(bf16)
    own_ref[...] = rows[:slots]
    for mask in range(1, experts):
        out_ref[mask - 1] = rows[slots + (mask - 1) * most : slots + mask * most]


def listed_rows(where, index, pool, experts, most, part):
    shard_rows, width = pool.shape
    slots = index.shape[1]
    steps = 2
    chunk = width // (2 * steps)
    return pl.pallas_call(
        functools.partial(listed_kernel, experts, most),
        out_shape=[
            jax.ShapeDtypeStruct((experts - 1, most, width // 2), bf16),
            jax.ShapeDtypeStruct((slots, width // 2), bf16),
        ],
        grid_spec=pltpu.PrefetchScalarGridSpec(
            num_scalar_prefetch=1,
            grid=(steps,),
            in_specs=[
                pl.BlockSpec(index.shape, lambda i, w: (0, 0)),
                pl.BlockSpec((shard_rows, chunk), lambda i, w: (0, (w[1] ^ 1 ^ part) * steps + i)),
            ],
            out_specs=[
                pl.BlockSpec((experts - 1, most, chunk), lambda i, w: (0, 0, i)),
                pl.BlockSpec((slots, chunk), lambda i, w: (0, i)),
            ],
            scratch_shapes=[pltpu.VMEM((slots + (experts - 1) * most, shard_rows), bf16)],
        ),
        compiler_params=params(),
        cost_estimate=LIGHT,
        name="listed_rows",
    )(where, index, pool)


def merge_kernel(experts, shard_rows, where_ref, index_ref, own_ref, *refs):
    incoming, out_ref = refs[: experts - 1], refs[experts - 1]
    me = where_ref[0]
    most = incoming[0].shape[1]
    block = out_ref.shape[2]
    listed = index_ref[pl.ds(me, 1), :]
    rows = own_ref[...].astype(f32)
    for mask in range(1, experts):
        pick = one_hot(slot_ranks(listed, me ^ mask, shard_rows), most)
        rows = rows + jnp.dot(pick, incoming[mask - 1][0], preferred_element_type=f32)
    rows = rows.astype(bf16)
    for column in range(out_ref.shape[0]):
        out_ref[column] = rows[:, column * block : (column + 1) * block]


def merged_rows(where, index, own, incoming, experts, replicas, shard_rows):
    slots, half = own.shape
    return pl.pallas_call(
        functools.partial(merge_kernel, experts, shard_rows),
        out_shape=jax.ShapeDtypeStruct((replicas // 2, slots, 2 * half // replicas), bf16),
        in_specs=[smem()] + [vmem()] * (experts + 1),
        out_specs=vmem(),
        compiler_params=params(),
        cost_estimate=LIGHT,
        name="merged_rows",
    )(where, index, own, *incoming)


def pack_kernel(masks, halves, where_ref, own_ref, peer_ref, *outs):
    upper, core = where_ref[2], where_ref[3]
    for mask, out in zip(masks, outs):
        first = ((upper ^ mask) & (halves - 1)) * 4
        for side in range(2):
            out[0, side] = own_ref[first + 2 * side + core]
            out[1, side] = peer_ref[first + 2 * side + core]


def packed_rows(where, own, peer, masks, halves):
    out = jax.ShapeDtypeStruct((2, 2) + own.shape[1:], bf16)
    return pl.pallas_call(
        functools.partial(pack_kernel, masks, halves),
        out_shape=[out] * len(masks),
        in_specs=[smem(), vmem(), vmem()],
        out_specs=[vmem()] * len(masks),
        compiler_params=params(),
        cost_estimate=LIGHT,
        name="packed_rows",
    )(where, own, peer)


def forward_kernel(uppers, where_ref, own_far, own_near, peer_far, peer_near, *refs):
    blocks, (own_out, peer_out) = refs[:4], refs[4:]
    upper, core, side = where_ref[2], where_ref[3], where_ref[4]
    own_value = jnp.zeros(own_out.shape, f32)
    peer_value = jnp.zeros(own_out.shape, f32)
    halves = uppers // 2
    for mask in range(uppers):
        own, peer = (own_far, peer_far) if mask >= halves else (own_near, peer_near)
        for side_mask in range(2):
            for core_mask in range(2):
                column = ((upper ^ mask) & (halves - 1)) * 4 + 2 * (side ^ side_mask) + (core ^ core_mask)
                w = blocks[2 * side_mask + (mask >= halves)][mask % halves, core_mask]
                own_value += jnp.dot(own[column], w, preferred_element_type=f32)
                peer_value += jnp.dot(peer[column], w, preferred_element_type=f32)
    own_out[...] = own_value
    peer_out[...] = peer_value


def forward(where, rows, blocks, uppers):
    out = jax.ShapeDtypeStruct((rows[0].shape[1], blocks[0].shape[3]), f32)
    return pl.pallas_call(
        functools.partial(forward_kernel, uppers),
        out_shape=[out, out],
        in_specs=[smem()] + [vmem()] * 8,
        out_specs=[vmem()] * 2,
        compiler_params=params(),
        cost_estimate=LIGHT,
        name="forward_values",
    )(where, *rows, *blocks)


def delta_kernel(where_ref, count_ref, targets_ref, own_ref, other_ref, kept_ref, sent_ref):
    core, side = where_ref[3], where_ref[4]
    slots = targets_ref.shape[0]
    gate_value = jnp.where(core == 0, own_ref[...], other_ref[...])
    up_value = jnp.where(core == 0, other_ref[...], own_ref[...])
    live_count = count_ref[0, 0]
    sigmoid = jax.nn.sigmoid(gate_value)
    activated = gate_value * sigmoid
    silu_slope = sigmoid * (1.0 + gate_value * (1.0 - sigmoid))
    live = (grid_iota((slots, 1), 0) < live_count).astype(f32)
    residual = (activated * up_value - targets_ref[...].astype(f32)) * live / jnp.full((1, 1), live_count, i32).astype(f32)
    gate_delta = (residual * up_value * silu_slope).astype(bf16)
    up_delta = (residual * activated).astype(bf16)
    kept_ref[...] = jnp.where(side == 0, gate_delta, up_delta)
    sent_ref[...] = jnp.where(side == 0, up_delta, gate_delta)


def deltas_of(where, count, targets, own, other):
    out = jax.ShapeDtypeStruct(targets.shape, bf16)
    return pl.pallas_call(
        delta_kernel,
        out_shape=[out, out],
        in_specs=[smem(), smem()] + [vmem()] * 3,
        out_specs=[vmem()] * 2,
        compiler_params=params(),
        cost_estimate=LIGHT,
        name="deltas",
    )(where, count, targets, own, other)


def token_contract(left, right):
    return lax.dot_general(left, right, (((0,), (0,)), ((), ())), preferred_element_type=f32)


TILE = 16


def split_refs(replicas, refs):
    uppers = replicas // 4
    own, near, far, rest = refs[:uppers], refs[uppers], refs[uppers + 1], refs[uppers + 2 :]

    def rows_of(upper, side):
        if side == 0:
            return own[upper]
        return near if upper == 0 else far.at[upper - 1]

    return rows_of, rest[:replicas], rest[replicas:]


def gram_kernel(replicas, where_ref, *refs):
    rows, deltas, (gram_ref, table_ref) = split_refs(replicas, refs)
    me = where_ref[5]
    block = refs[0].shape[3]
    steps = block // TILE
    for mask in range(replicas):
        first = pl.multiple_of((me ^ mask) * TILE, TILE)
        upper, side, core = mask >> 2, mask >> 1 & 1, mask & 1
        for part in range(2):
            gradient = token_contract(rows(upper, side)[core, part], deltas[mask][...]).astype(bf16)
            for step in range(steps):
                table_ref[part * steps + step, pl.ds(first, TILE), :] = gradient[step * TILE : (step + 1) * TILE]
    size = replicas * TILE
    products = jnp.zeros((size, size), f32)
    for step in range(2 * steps):
        products += lax.dot_general(
            table_ref[step], table_ref[step], (((1,), (1,)), ((), ())), preferred_element_type=f32
        )
    same = (grid_iota((size, size), 0) & (TILE - 1)) == (grid_iota((size, size), 1) & (TILE - 1))
    products = jnp.where(same, products, 0.0)
    down = jnp.concatenate(
        [jnp.sum(products[r * TILE : (r + 1) * TILE], axis=0, keepdims=True) for r in range(replicas)], axis=0
    )
    member = (grid_iota((size, replicas), 0) // TILE == grid_iota((size, replicas), 1)).astype(f32)
    gram_ref[...] = jnp.dot(down, member, preferred_element_type=f32, precision=lax.Precision.HIGHEST)


def gram(where, rows, deltas, replicas):
    depth = 2 * rows[0].shape[3]
    hidden = deltas[0].shape[1]
    return pl.pallas_call(
        functools.partial(gram_kernel, replicas),
        out_shape=jax.ShapeDtypeStruct((replicas, replicas), f32),
        in_specs=[smem()] + [vmem()] * (len(rows) + len(deltas)),
        out_specs=vmem(),
        scratch_shapes=[pltpu.VMEM((depth // TILE, replicas * TILE, hidden), bf16)],
        compiler_params=params(),
        cost_estimate=LIGHT,
        name="gradient_products",
    )(where, *rows, *deltas)


def tree_weights(table, replicas):
    down, along = grid_iota((replicas, replicas), 0), grid_iota((replicas, replicas), 1)
    weights = jnp.ones((replicas, 1), f32)
    half = replicas // 2
    while half >= 1:
        same = down == along
        other = ((down + half) & (replicas - 1)) == along
        partner = ((along + half) & (replicas - 1)) == down
        square_down = jnp.sum(jnp.where(same, table, 0.0), axis=1, keepdims=True)
        square_along = jnp.sum(jnp.where(same, table, 0.0), axis=0, keepdims=True)
        inner_down = jnp.sum(jnp.where(other, table, 0.0), axis=1, keepdims=True)
        inner_along = jnp.sum(jnp.where(partner, table, 0.0), axis=0, keepdims=True)
        weight_down = 1.0 - inner_down / (2.0 * square_down + adasum_epsilon)
        weight_along = 1.0 - inner_along / (2.0 * square_along + adasum_epsilon)
        weights = weights * weight_down
        table = weight_down * (table * weight_along)
        table = table + jnp.concatenate([table[half:], table[:half]], axis=0)
        table = table + jnp.concatenate([table[:, half:], table[:, :half]], axis=1)
        half //= 2
    return weights


def combine_kernel(replicas, where_ref, gram_ref, *refs):
    rows, deltas, (kept_ref, sent_ref, weight_ref) = split_refs(replicas, refs)
    side, me = where_ref[4], where_ref[5]
    weight_ref[...] = jnp.broadcast_to(tree_weights(gram_ref[...], replicas), weight_ref.shape)
    for ref, part in ((kept_ref, side), (sent_ref, 1 - side)):
        total = jnp.zeros(ref.shape, f32)
        for mask in range(replicas):
            upper, side_mask, core = mask >> 2, mask >> 1 & 1, mask & 1
            gradient = token_contract(rows(upper, side_mask)[core, part], deltas[mask][...])
            total = total + weight_ref[pl.ds(me ^ mask, 1), 0:1] * gradient
        ref[...] = total


def combine(where, products, rows, deltas):
    replicas = products.shape[0]
    out = jax.ShapeDtypeStruct((rows[0].shape[3], deltas[0].shape[1]), f32)
    return pl.pallas_call(
        functools.partial(combine_kernel, replicas),
        out_shape=[out, out],
        in_specs=[smem(), vmem()] + [vmem()] * (len(rows) + len(deltas)),
        out_specs=[vmem()] * 2,
        scratch_shapes=[pltpu.VMEM((replicas, 128), f32)],
        compiler_params=params(),
        cost_estimate=LIGHT,
        name="combined_gradient",
    )(where, products, *rows, *deltas)


def shards(pool, row_index, counts, targets, weights, first_moment, second_moment):
    replicas = lax.axis_size("replica")
    experts = lax.axis_size("expert")
    uppers = replicas // 4
    position = lax.axis_index("replica")
    expert_position = lax.axis_index("expert")
    core, side, upper = position & 1, position >> 1 & 1, position >> 2
    where = jnp.stack([expert_position, position // (replicas // 2), upper, core, side, position]).astype(i32)
    index = row_index[:, 0, :]
    local_pool = pool[0]
    shard_rows = local_pool.shape[0]
    most = 3 * index.shape[1] // (2 * experts)

    lowered = weights[0].astype(bf16)
    mine = jnp.where(core == 0, lowered[0], lowered[1])
    others = swapped(jnp.where(core == 0, lowered[1], lowered[0]), "replica", CORE)
    pair = jnp.stack([mine, others])
    upper_masks = [4 << bit for bit in range(uppers.bit_length() - 1)]
    by_upper = gathered(pair, upper_masks)
    by_upper = [by_upper[4 * mask] for mask in range(uppers)]
    blocks = [jnp.stack(by_upper[: uppers // 2]), jnp.stack(by_upper[uppers // 2 :])]
    blocks += [swapped(block, "replica", SIDE) for block in blocks]

    halves = uppers // 2
    incoming, own = [], []
    for part in range(2):
        if part == 1:
            where, pair = lax.optimization_barrier((where, pair))
        outgoing, owned = listed_rows(where, index, local_pool, experts, most, part)
        own.append(owned)
        incoming.append(
            [swapped(outgoing[mask - 1 : mask], "expert", mask) for mask in range(1, experts)]
        )
    here, packed = [], [None] * uppers
    for part in range(2):
        masks = list(range(halves, uppers)) if part == 0 else list(range(halves))
        merged = merged_rows(where, index, own[part], incoming[part], experts, replicas, shard_rows)
        peer = swapped(merged, "replica", CORE)
        here.append((merged, peer))
        for mask, piece in zip(masks, packed_rows(where, merged, peer, masks, halves)):
            packed[mask] = piece
    for mask in list(range(halves, uppers)) + list(range(1, halves)):
        packed[mask] = swapped(packed[mask], "replica", 4 * mask)
    here, packed[1] = lax.optimization_barrier((here, packed[1]))

    own_value, peer_value = forward(
        where, (here[0][0], here[1][0], here[0][1], here[1][1]), blocks, uppers
    )
    other_value = swapped(peer_value, "replica", CORE)
    own_value, *packed = lax.optimization_barrier((own_value, *packed))
    kept_delta, sent_delta = deltas_of(where, counts, targets[0, 0], own_value, other_value)
    side_deltas = [kept_delta, swapped(sent_delta, "replica", SIDE)]

    beside = swapped(packed[0], "replica", SIDE)
    others, _ = lax.optimization_barrier((jnp.stack(packed[1:]), kept_delta))
    rows = packed + [beside, swapped(others, "replica", SIDE)]
    deltas = [None] * replicas
    for side_mask, own_delta in enumerate(side_deltas):
        for mask, piece in gathered(own_delta, upper_masks).items():
            deltas[mask + 2 * side_mask] = piece
            deltas[mask + 2 * side_mask + 1] = swapped(piece, "replica", CORE)

    products = gram(where, rows, deltas, replicas)
    products = products + swapped(products, "replica", CORE)
    mask = 4
    while mask < replicas:
        products = products + swapped(products, "replica", mask)
        mask *= 2
    kept_block, sent_block = combine(where, products, rows, deltas)
    other_block = swapped(sent_block, "replica", SIDE)
    combined = jnp.where(
        side == 0, jnp.stack([kept_block, other_block]), jnp.stack([other_block, kept_block])
    )
    new_weight, moment_one, moment_two = adam_update(
        combined, weights[0], first_moment[0], second_moment[0]
    )
    return (new_weight[None], moment_one[None], moment_two[None])


def solution(mesh):
    in_specs = (
        P("replica", "expert", None),
        P(None, "replica", None),
        P("expert", "replica"),
        P("expert", "replica", None, None),
        P("expert", None, "replica", None),
        P("expert", None, "replica", None),
        P("expert", None, "replica", None),
    )
    out_specs = (
        P("expert", None, "replica", None),
        P("expert", None, "replica", None),
        P("expert", None, "replica", None),
    )
    return jax.shard_map(shards, mesh=mesh, in_specs=in_specs, out_specs=out_specs, check_vma=False)
```

```python
import functools
import math

import jax
import jax.numpy as jnp
from jax import lax
from jax.experimental import pallas as pl
from jax.experimental.pallas import tpu as pltpu
from jax.sharding import PartitionSpec as P

STEP = 3


beta_first = 0.9
beta_second = 0.999
learning_rate = 0.02
decay_rate = 0.1
adam_epsilon = 1e-08
adasum_epsilon = 1e-12

CORE, SIDE = 1, 2
VMEM_LIMIT = 50 * 1024 * 1024
LIGHT = pl.CostEstimate(flops=1, bytes_accessed=1, transcendentals=0)
f32, bf16, i32 = jnp.float32, jnp.bfloat16, jnp.int32


def gathered(x, masks):
    pieces = {0: x}
    for mask in reversed(masks):
        pieces.update({mask | held: swapped(piece, "replica", mask) for held, piece in list(pieces.items())})
    return pieces


def swapped(x, axis, mask):
    return lax.ppermute(x, axis, [(i, i ^ mask) for i in range(lax.axis_size(axis))])


def vmem():
    return pl.BlockSpec(memory_space=pltpu.VMEM)


def smem():
    return pl.BlockSpec(memory_space=pltpu.SMEM)


def params(*arrays):
    total = 0
    for array in arrays:
        *lead, rows, columns = array.shape
        total += math.prod(lead) * -(-rows // 16) * 16 * -(-columns // 128) * 128 * array.dtype.itemsize
    return pltpu.CompilerParams(vmem_limit_bytes=min(2 * total + 4 * 1024 * 1024, VMEM_LIMIT))


def adam_update(gradient, weight, moment_one, moment_two):
    moment_one = beta_first * moment_one + (1.0 - beta_first) * gradient
    moment_two = beta_second * moment_two + (1.0 - beta_second) * gradient * gradient
    first_hat = moment_one / (1.0 - beta_first**STEP)
    second_hat = moment_two / (1.0 - beta_second**STEP)
    weight = weight - learning_rate * (
        first_hat / (jnp.sqrt(second_hat) + adam_epsilon) + decay_rate * weight
    )
    return (weight, moment_one, moment_two)


def grid_iota(shape, dim):
    return lax.broadcasted_iota(i32, shape, dim)


def compacted_rows(listed, block, shard_rows, most):
    slots = listed.shape[1]
    local = listed - block * shard_rows
    held = (local >= 0) & (local < shard_rows)
    down, along = grid_iota((slots, slots), 0), grid_iota((slots, slots), 1)
    held_wide = jnp.broadcast_to(held.astype(i32), (slots, slots))
    held_column = jnp.sum(jnp.where(down == along, held_wide, 0), axis=1, keepdims=True)
    rank = jnp.sum(jnp.where(down < along, jnp.broadcast_to(held_column, (slots, slots)), 0), axis=0, keepdims=True)
    place = jnp.where(held, rank, -1)
    hit = grid_iota((most, slots), 0) == jnp.broadcast_to(place, (most, slots))
    return jnp.sum(jnp.where(hit, jnp.broadcast_to(local + 1, (most, slots)), 0), axis=1, keepdims=True) - 1


def slot_rows(listed, block, shard_rows):
    slots = listed.shape[1]
    local = listed - block * shard_rows
    held = (local >= 0) & (local < shard_rows)
    value = jnp.where(held, local + 1, 0)
    diagonal = grid_iota((slots, slots), 0) == grid_iota((slots, slots), 1)
    return jnp.sum(jnp.where(diagonal, jnp.broadcast_to(value, (slots, slots)), 0), axis=1, keepdims=True) - 1


def slot_ranks(listed, block, shard_rows):
    slots = listed.shape[1]
    local = listed - block * shard_rows
    held = ((local >= 0) & (local < shard_rows)).astype(i32)
    held_wide = jnp.broadcast_to(held, (slots, slots))
    down, along = grid_iota((slots, slots), 0), grid_iota((slots, slots), 1)
    rank = jnp.sum(jnp.where(along < down, held_wide, 0), axis=1, keepdims=True)
    own = jnp.sum(jnp.where(along == down, held_wide, 0), axis=1, keepdims=True)
    return jnp.where(own > 0, rank, -1)


def one_hot(column, width):
    return (grid_iota((column.shape[0], width), 1) == column).astype(f32).astype(bf16)


def pick_kernel(experts, most, shard_rows, where_ref, index_ref, pick_ref):
    slots = index_ref.shape[1]
    me = where_ref[0]
    pick_ref[:slots] = one_hot(slot_rows(index_ref[pl.ds(me, 1), :], me, shard_rows), shard_rows)
    for mask in range(1, experts):
        listed = index_ref[pl.ds(me ^ mask, 1), :]
        first = slots + (mask - 1) * most
        pick_ref[first : first + most] = one_hot(compacted_rows(listed, me, shard_rows, most), shard_rows)


def picks_of(where, index, experts, most, shard_rows):
    return pl.pallas_call(
        functools.partial(pick_kernel, experts, most, shard_rows),
        out_shape=jax.ShapeDtypeStruct((index.shape[1] + (experts - 1) * most, shard_rows), bf16),
        in_specs=[smem(), vmem()],
        out_specs=vmem(),
        compiler_params=params(jax.ShapeDtypeStruct((2 * most, shard_rows), f32)),
        cost_estimate=LIGHT,
        name="row_picks",
    )(where, index)


def listed_kernel(experts, most, where_ref, pick_ref, pool_ref, out_ref, own_ref):
    slots = own_ref.shape[0]
    rows = jnp.dot(pick_ref[...], pool_ref[...], preferred_element_type=f32).astype(bf16)
    own_ref[...] = rows[:slots]
    for mask in range(1, experts):
        out_ref[mask - 1] = rows[slots + (mask - 1) * most : slots + mask * most]


def listed_rows(where, picks, pool, experts, most, part):
    shard_rows, width = pool.shape
    slots = picks.shape[0] - (experts - 1) * most
    steps = 4 if width // 8 % 128 == 0 else 2
    chunk = width // (2 * steps)
    return pl.pallas_call(
        functools.partial(listed_kernel, experts, most),
        out_shape=[
            jax.ShapeDtypeStruct((experts - 1, most, width // 2), bf16),
            jax.ShapeDtypeStruct((slots, width // 2), bf16),
        ],
        grid_spec=pltpu.PrefetchScalarGridSpec(
            num_scalar_prefetch=1,
            grid=(steps,),
            in_specs=[
                pl.BlockSpec(picks.shape, lambda i, w: (0, 0)),
                pl.BlockSpec((shard_rows, chunk), lambda i, w: (0, (w[1] ^ 1 ^ part) * steps + i)),
            ],
            out_specs=[
                pl.BlockSpec((experts - 1, most, chunk), lambda i, w: (0, 0, i)),
                pl.BlockSpec((slots, chunk), lambda i, w: (0, i)),
            ],
        ),
        compiler_params=pltpu.CompilerParams(vmem_limit_bytes=VMEM_LIMIT),
        cost_estimate=LIGHT,
        name="listed_rows",
    )(where, picks, pool)


def merge_kernel(experts, shard_rows, masks, halves, where_ref, index_ref, own_ref, *refs):
    incoming, sent_refs, block_ref = refs[: experts - 1], refs[experts - 1 : -1], refs[-1]
    me, upper, core = where_ref[0], where_ref[2], where_ref[3]
    most = incoming[0].shape[1]
    block = block_ref.shape[2]
    listed = index_ref[pl.ds(me, 1), :]
    rows = own_ref[...].astype(f32)
    for mask in range(1, experts):
        pick = one_hot(slot_ranks(listed, me ^ mask, shard_rows), most)
        rows = rows + jnp.dot(pick, incoming[mask - 1][0], preferred_element_type=f32)
    rows = rows.astype(bf16)
    for column in range(block_ref.shape[0]):
        block_ref[column] = rows[:, column * block : (column + 1) * block]
    for mask, sent_ref in zip(masks, sent_refs):
        first = ((upper ^ mask) & (halves - 1)) * 4
        for core_mask in range(2):
            for side in range(2):
                sent_ref[core_mask, side] = block_ref[first + 2 * side + (core ^ core_mask)]


def merged_rows(where, index, own, incoming, experts, replicas, shard_rows, masks):
    slots, half = own.shape
    block = 2 * half // replicas
    return pl.pallas_call(
        functools.partial(merge_kernel, experts, shard_rows, masks, replicas // 8),
        out_shape=[jax.ShapeDtypeStruct((2, 2, slots, block), bf16)] * len(masks),
        in_specs=[smem()] + [vmem()] * (experts + 1),
        out_specs=[vmem()] * len(masks),
        scratch_shapes=[pltpu.VMEM((replicas // 2, slots, block), bf16)],
        compiler_params=params(own, own, own, *incoming),
        cost_estimate=LIGHT,
        name="merged_rows",
    )(where, index, own, *incoming)


def forward_kernel(uppers, blocks, where_ref, crossed_ref, *refs):
    own, rest, outs = refs[:uppers], refs[uppers:], refs[uppers + len(blocks.arrays) :]
    side = where_ref[4]
    totals = [jnp.zeros(out.shape, f32) for out in outs]
    for mask in range(uppers):
        peer = crossed_ref.at[mask]
        for side_mask in range(2):
            w = blocks.ref(rest, 4 * mask + 2 * side_mask)
            for rows, first in ((own[mask].at[0], 0), (peer, 2)):
                for matrix in range(2):
                    totals[first + matrix] += jnp.dot(rows[side ^ side_mask], w[matrix], preferred_element_type=f32)
    for out, total in zip(outs, totals):
        out[...] = total


def forward(where, crossed, own, blocks, uppers):
    out = jax.ShapeDtypeStruct((crossed.shape[2], blocks.arrays[0].shape[2]), f32)
    return pl.pallas_call(
        functools.partial(forward_kernel, uppers, blocks),
        out_shape=[out] * 4,
        in_specs=[smem()] + [vmem()] * (1 + uppers + len(blocks.arrays)),
        out_specs=[vmem()] * 4,
        compiler_params=params(crossed, *own, *blocks.arrays),
        cost_estimate=LIGHT,
        name="forward_values",
    )(where, crossed, *own, *blocks.arrays)


def delta_kernel(where_ref, count_ref, targets_ref, gate_ref, up_ref, gate_other_ref, up_other_ref, kept_ref, sent_ref):
    side = where_ref[4]
    slots = targets_ref.shape[0]
    gate_value = gate_ref[...] + gate_other_ref[...]
    up_value = up_ref[...] + up_other_ref[...]
    live_count = count_ref[0, 0]
    sigmoid = jax.nn.sigmoid(gate_value)
    activated = gate_value * sigmoid
    silu_slope = sigmoid * (1.0 + gate_value * (1.0 - sigmoid))
    live = (grid_iota((slots, 1), 0) < live_count).astype(f32)
    residual = (activated * up_value - targets_ref[...].astype(f32)) * live / jnp.full((1, 1), live_count, i32).astype(f32)
    gate_delta = (residual * up_value * silu_slope).astype(bf16)
    up_delta = (residual * activated).astype(bf16)
    kept_ref[...] = jnp.where(side == 0, gate_delta, up_delta)
    sent_ref[...] = jnp.where(side == 0, up_delta, gate_delta)


def deltas_of(where, count, targets, values):
    out = jax.ShapeDtypeStruct(targets.shape, bf16)
    return pl.pallas_call(
        delta_kernel,
        out_shape=[out, out],
        in_specs=[smem(), smem()] + [vmem()] * 5,
        out_specs=[vmem()] * 2,
        compiler_params=params(targets, *values),
        cost_estimate=LIGHT,
        name="deltas",
    )(where, count, targets, *values)


def token_contract(left, right):
    return lax.dot_general(left, right, (((0,), (0,)), ((), ())), preferred_element_type=f32)


TILE = 16


class Pieces:
    def __init__(self):
        self.arrays, self.place = [], {}

    def put(self, keys, pieces):
        if isinstance(pieces, list):
            for key, piece in zip(keys, pieces):
                self.place[key] = (len(self.arrays), None)
                self.arrays.append(piece)
            return
        for index, key in enumerate(keys):
            self.place[key] = (len(self.arrays), index)
        self.arrays.append(pieces)

    def ref(self, refs, key):
        array, index = self.place[key]
        return refs[array] if index is None else refs[array].at[index]

    def read(self, refs, key):
        return self.ref(refs, key)[...]


def split_refs(rows, deltas, refs):
    count = len(rows.arrays)
    rest = refs[count:]

    def rows_of(key):
        ref = rows.ref(refs, key)
        return ref.at[0] if len(ref.shape) == 4 else ref

    return rows_of, lambda key: deltas.read(rest, key), rest[len(deltas.arrays) :]


def gram_kernel(replicas, pieces, where_ref, *refs):
    rows, deltas, (gram_ref, table_ref) = split_refs(*pieces, refs)
    me = where_ref[5]
    block = rows(0).shape[2]
    steps = block // TILE
    for mask in range(replicas):
        first = pl.multiple_of((me ^ mask) * TILE, TILE)
        for part in range(2):
            gradient = token_contract(rows(mask)[part], deltas(mask)).astype(bf16)
            for step in range(steps):
                table_ref[part * steps + step, pl.ds(first, TILE), :] = gradient[step * TILE : (step + 1) * TILE]
    size = replicas * TILE
    products = jnp.zeros((size, size), f32)
    for step in range(2 * steps):
        products += lax.dot_general(
            table_ref[step], table_ref[step], (((1,), (1,)), ((), ())), preferred_element_type=f32
        )
    same = (grid_iota((size, size), 0) & (TILE - 1)) == (grid_iota((size, size), 1) & (TILE - 1))
    products = jnp.where(same, products, 0.0)
    down = jnp.concatenate(
        [jnp.sum(products[r * TILE : (r + 1) * TILE], axis=0, keepdims=True) for r in range(replicas)], axis=0
    )
    member = (grid_iota((size, replicas), 0) // TILE == grid_iota((size, replicas), 1)).astype(f32)
    gram_ref[...] = jnp.dot(down, member, preferred_element_type=f32, precision=lax.Precision.HIGHEST)


def gram(where, rows, deltas, replicas):
    depth = 2 * rows.arrays[0].shape[-1]
    hidden = deltas.arrays[0].shape[-1]
    return pl.pallas_call(
        functools.partial(gram_kernel, replicas, (rows, deltas)),
        out_shape=jax.ShapeDtypeStruct((replicas, replicas), f32),
        in_specs=[smem()] + [vmem()] * (len(rows.arrays) + len(deltas.arrays)),
        out_specs=vmem(),
        scratch_shapes=[pltpu.VMEM((depth // TILE, replicas * TILE, hidden), bf16)],
        compiler_params=params(*rows.arrays, *deltas.arrays, jax.ShapeDtypeStruct((replicas * TILE, replicas * TILE), f32)),
        cost_estimate=LIGHT,
        name="gradient_products",
    )(where, *rows.arrays, *deltas.arrays)


def tree_weights(table, replicas):
    down, along = grid_iota((replicas, replicas), 0), grid_iota((replicas, replicas), 1)
    weights = jnp.ones((replicas, 1), f32)
    half = replicas // 2
    while half >= 1:
        same = down == along
        other = ((down + half) & (replicas - 1)) == along
        partner = ((along + half) & (replicas - 1)) == down
        square_down = jnp.sum(jnp.where(same, table, 0.0), axis=1, keepdims=True)
        square_along = jnp.sum(jnp.where(same, table, 0.0), axis=0, keepdims=True)
        inner_down = jnp.sum(jnp.where(other, table, 0.0), axis=1, keepdims=True)
        inner_along = jnp.sum(jnp.where(partner, table, 0.0), axis=0, keepdims=True)
        weight_down = 1.0 - inner_down / (2.0 * square_down + adasum_epsilon)
        weight_along = 1.0 - inner_along / (2.0 * square_along + adasum_epsilon)
        weights = weights * weight_down
        table = weight_down * (table * weight_along)
        table = table + jnp.concatenate([table[half:], table[:half]], axis=0)
        table = table + jnp.concatenate([table[:, half:], table[:, :half]], axis=1)
        half //= 2
    return weights


def combine_kernel(replicas, pieces, where_ref, gram_ref, *refs):
    rows, deltas, (kept_ref, sent_ref, weight_ref) = split_refs(*pieces, refs)
    side, me = where_ref[4], where_ref[5]
    weight_ref[...] = jnp.broadcast_to(tree_weights(gram_ref[...], replicas), weight_ref.shape)
    for ref, part in ((kept_ref, side), (sent_ref, 1 - side)):
        total = jnp.zeros(ref.shape, f32)
        for mask in range(replicas):
            gradient = token_contract(rows(mask)[part], deltas(mask))
            total = total + weight_ref[pl.ds(me ^ mask, 1), 0:1] * gradient
        ref[...] = total


def combine(where, products, rows, deltas):
    replicas = products.shape[0]
    out = jax.ShapeDtypeStruct((rows.arrays[0].shape[-1], deltas.arrays[0].shape[-1]), f32)
    return pl.pallas_call(
        functools.partial(combine_kernel, replicas, (rows, deltas)),
        out_shape=[out, out],
        in_specs=[smem(), vmem()] + [vmem()] * (len(rows.arrays) + len(deltas.arrays)),
        out_specs=[vmem()] * 2,
        scratch_shapes=[pltpu.VMEM((replicas, 128), f32)],
        compiler_params=params(*rows.arrays, *deltas.arrays),
        cost_estimate=LIGHT,
        name="combined_gradient",
    )(where, products, *rows.arrays, *deltas.arrays)


def shards(pool, row_index, counts, targets, weights, first_moment, second_moment):
    replicas = lax.axis_size("replica")
    experts = lax.axis_size("expert")
    uppers = replicas // 4
    position = lax.axis_index("replica")
    expert_position = lax.axis_index("expert")
    core, side, upper = position & 1, position >> 1 & 1, position >> 2
    where = jnp.stack([expert_position, position // (replicas // 2), upper, core, side, position]).astype(i32)
    index = row_index[:, 0, :]
    local_pool = pool[0]
    shard_rows = local_pool.shape[0]
    most = 3 * index.shape[1] // (2 * experts)

    halves = uppers // 2
    upper_masks = [4 << bit for bit in range(uppers.bit_length() - 1)]
    picks = picks_of(where, index, experts, most, shard_rows)
    far, near = list(range(halves, uppers)), list(range(halves))
    packed = [None] * uppers
    for part, masks in enumerate((far, near)):
        outgoing, own = listed_rows(where, picks, local_pool, experts, most, part)
        incoming = [swapped(outgoing[mask - 1 : mask], "expert", mask) for mask in range(1, experts)]
        if part == 0:
            lowered = weights[0].astype(bf16)
            by_upper = gathered(lowered, upper_masks)
            by_upper = [by_upper[4 * mask] for mask in range(uppers)]
            own, picks, *_ = lax.optimization_barrier((own, picks, by_upper[halves], by_upper[1]))
        packed[masks[0] : masks[-1] + 1] = merged_rows(
            where, index, own, incoming, experts, replicas, shard_rows, masks
        )

    crossed = swapped(jnp.stack([piece[1] for piece in packed]), "replica", CORE)

    direct = [0] + [1 << bit for bit in range(len(upper_masks))]
    relayed = [mask for mask in range(uppers) if mask not in direct]
    beside_direct = swapped(jnp.stack([by_upper[mask] for mask in direct]), "replica", SIDE)
    beside_relayed = [swapped(by_upper[mask], "replica", SIDE) for mask in relayed]
    blocks = Pieces()
    blocks.put([4 * mask for mask in range(uppers)], by_upper)
    blocks.put([4 * mask | SIDE for mask in direct], beside_direct)
    blocks.put([4 * mask | SIDE for mask in relayed], beside_relayed)
    values = forward(where, crossed, packed, blocks, uppers)

    rows = Pieces()
    rows.put([0], [packed[0]])
    others_of = far + near[1:]
    arrived = [swapped(packed[mask], "replica", 4 * mask) for mask in others_of]
    other = swapped(jnp.stack([piece[1] for piece in arrived]), "replica", CORE)
    for mask, piece in zip(others_of, arrived):
        rows.put([4 * mask], [piece])
    rows.put([4 * mask | CORE for mask in others_of], other)
    rows.put([CORE], crossed)
    values = list(values[:2]) + [swapped(value, "replica", CORE) for value in values[2:]]
    kept_delta, sent_delta = deltas_of(where, counts, targets[0, 0], values)
    side_deltas = [kept_delta, swapped(sent_delta, "replica", SIDE)]

    deltas = Pieces()
    far_mask, near_masks = upper_masks[-1], upper_masks[:-1]

    def hold(keys, pieces):
        both = jnp.stack(pieces)
        deltas.put(keys, both)
        across = swapped(both, "replica", CORE)
        deltas.put([key | CORE for key in keys], across)
        return both, across

    hold([0, SIDE], side_deltas)
    kept_far = swapped(kept_delta, "replica", far_mask)
    kept_near, beside_near = [gathered(piece, near_masks) for piece in side_deltas]
    keys = [mask for mask in kept_near if mask > 0]
    kept_near, beside_near = [kept_near[key] for key in keys], [beside_near[key] for key in keys]
    beside_own, *_ = lax.optimization_barrier((side_deltas[1], *kept_near))
    beside_far = swapped(beside_own, "replica", far_mask)
    all_here = [packed[0][0]] + [piece[0] for piece in arrived] + [crossed[0]] + [other[i] for i in range(len(arrived))]
    all_here, _ = lax.optimization_barrier((jnp.stack(all_here), side_deltas[1]))
    keys_beside = [4 * mask | SIDE for mask in [0] + others_of]
    rows.put(keys_beside + [key | CORE for key in keys_beside], swapped(all_here, "replica", SIDE))
    hold(keys + [key | SIDE for key in keys], kept_near + beside_near)
    far, _ = hold([far_mask, far_mask | SIDE], [kept_far, beside_far])
    far, *_ = lax.optimization_barrier((far, *kept_near, *beside_near))
    for key, piece in gathered(far, near_masks).items():
        if key > 0:
            keys = [far_mask | key, far_mask | key | SIDE]
            deltas.put(keys, piece)
            deltas.put([key | CORE for key in keys], swapped(piece, "replica", CORE))

    products = gram(where, rows, deltas, replicas)
    products = products + swapped(products, "replica", CORE)
    mask = 4
    while mask < replicas:
        products = products + swapped(products, "replica", mask)
        mask *= 2
    kept_block, sent_block = combine(where, products, rows, deltas)
    other_block = swapped(sent_block, "replica", SIDE)
    combined = jnp.where(
        side == 0, jnp.stack([kept_block, other_block]), jnp.stack([other_block, kept_block])
    )
    new_weight, moment_one, moment_two = adam_update(
        combined, weights[0], first_moment[0], second_moment[0]
    )
    return (new_weight[None], moment_one[None], moment_two[None])


def solution(mesh):
    in_specs = (
        P("replica", "expert", None),
        P(None, "replica", None),
        P("expert", "replica"),
        P("expert", "replica", None, None),
        P("expert", None, "replica", None),
        P("expert", None, "replica", None),
        P("expert", None, "replica", None),
    )
    out_specs = (
        P("expert", None, "replica", None),
        P("expert", None, "replica", None),
        P("expert", None, "replica", None),
    )
    return jax.shard_map(shards, mesh=mesh, in_specs=in_specs, out_specs=out_specs, check_vma=False)
```

```python
import functools
import math

import jax
import jax.numpy as jnp
from jax import lax
from jax.experimental import pallas as pl
from jax.experimental.pallas import tpu as pltpu
from jax.sharding import PartitionSpec as P

STEP = 3


beta_first = 0.9
beta_second = 0.999
learning_rate = 0.02
decay_rate = 0.1
adam_epsilon = 1e-08
adasum_epsilon = 1e-12

CORE, SIDE = 1, 2
VMEM_LIMIT = 50 * 1024 * 1024
LIGHT = pl.CostEstimate(flops=1, bytes_accessed=1, transcendentals=0)
f32, bf16, i32 = jnp.float32, jnp.bfloat16, jnp.int32


def gathered(x, masks):
    pieces = {0: x}
    for mask in reversed(masks):
        pieces.update({mask | held: swapped(piece, "replica", mask) for held, piece in list(pieces.items())})
    return pieces


def swapped(x, axis, mask):
    return lax.ppermute(x, axis, [(i, i ^ mask) for i in range(lax.axis_size(axis))])


def vmem():
    return pl.BlockSpec(memory_space=pltpu.VMEM)


def smem():
    return pl.BlockSpec(memory_space=pltpu.SMEM)


def params(*arrays):
    total = 0
    for array in arrays:
        *lead, rows, columns = array.shape
        total += math.prod(lead) * -(-rows // 16) * 16 * -(-columns // 128) * 128 * array.dtype.itemsize
    return pltpu.CompilerParams(vmem_limit_bytes=min(2 * total + 4 * 1024 * 1024, VMEM_LIMIT))


def adam_update(gradient, weight, moment_one, moment_two):
    moment_one = beta_first * moment_one + (1.0 - beta_first) * gradient
    moment_two = beta_second * moment_two + (1.0 - beta_second) * gradient * gradient
    first_hat = moment_one / (1.0 - beta_first**STEP)
    second_hat = moment_two / (1.0 - beta_second**STEP)
    weight = weight - learning_rate * (
        first_hat / (jnp.sqrt(second_hat) + adam_epsilon) + decay_rate * weight
    )
    return (weight, moment_one, moment_two)


def grid_iota(shape, dim):
    return lax.broadcasted_iota(i32, shape, dim)


def compacted_rows(listed, block, shard_rows, most):
    slots = listed.shape[1]
    local = listed - block * shard_rows
    held = (local >= 0) & (local < shard_rows)
    down, along = grid_iota((slots, slots), 0), grid_iota((slots, slots), 1)
    held_wide = jnp.broadcast_to(held.astype(i32), (slots, slots))
    held_column = jnp.sum(jnp.where(down == along, held_wide, 0), axis=1, keepdims=True)
    rank = jnp.sum(jnp.where(down < along, jnp.broadcast_to(held_column, (slots, slots)), 0), axis=0, keepdims=True)
    place = jnp.where(held, rank, -1)
    hit = grid_iota((most, slots), 0) == jnp.broadcast_to(place, (most, slots))
    return jnp.sum(jnp.where(hit, jnp.broadcast_to(local + 1, (most, slots)), 0), axis=1, keepdims=True) - 1


def slot_rows(listed, block, shard_rows):
    slots = listed.shape[1]
    local = listed - block * shard_rows
    held = (local >= 0) & (local < shard_rows)
    value = jnp.where(held, local + 1, 0)
    diagonal = grid_iota((slots, slots), 0) == grid_iota((slots, slots), 1)
    return jnp.sum(jnp.where(diagonal, jnp.broadcast_to(value, (slots, slots)), 0), axis=1, keepdims=True) - 1


def slot_ranks(listed, block, shard_rows):
    slots = listed.shape[1]
    local = listed - block * shard_rows
    held = ((local >= 0) & (local < shard_rows)).astype(i32)
    held_wide = jnp.broadcast_to(held, (slots, slots))
    down, along = grid_iota((slots, slots), 0), grid_iota((slots, slots), 1)
    rank = jnp.sum(jnp.where(along < down, held_wide, 0), axis=1, keepdims=True)
    own = jnp.sum(jnp.where(along == down, held_wide, 0), axis=1, keepdims=True)
    return jnp.where(own > 0, rank, -1)


def one_hot(column, width):
    return (grid_iota((column.shape[0], width), 1) == column).astype(f32).astype(bf16)


def pick_kernel(experts, most, shard_rows, where_ref, index_ref, pick_ref):
    slots = index_ref.shape[1]
    me = where_ref[0]
    pick_ref[:slots] = one_hot(slot_rows(index_ref[pl.ds(me, 1), :], me, shard_rows), shard_rows)
    for mask in range(1, experts):
        listed = index_ref[pl.ds(me ^ mask, 1), :]
        first = slots + (mask - 1) * most
        pick_ref[first : first + most] = one_hot(compacted_rows(listed, me, shard_rows, most), shard_rows)


def picks_of(where, index, experts, most, shard_rows):
    return pl.pallas_call(
        functools.partial(pick_kernel, experts, most, shard_rows),
        out_shape=jax.ShapeDtypeStruct((index.shape[1] + (experts - 1) * most, shard_rows), bf16),
        in_specs=[smem(), vmem()],
        out_specs=vmem(),
        compiler_params=params(jax.ShapeDtypeStruct((2 * most, shard_rows), f32)),
        cost_estimate=LIGHT,
        name="row_picks",
    )(where, index)


def listed_kernel(experts, most, where_ref, pick_ref, pool_ref, out_ref, own_ref):
    slots = own_ref.shape[0]
    rows = jnp.dot(pick_ref[...], pool_ref[...], preferred_element_type=f32).astype(bf16)
    own_ref[...] = rows[:slots]
    for mask in range(1, experts):
        out_ref[mask - 1] = rows[slots + (mask - 1) * most : slots + mask * most]


def listed_rows(where, picks, pool, experts, most, part):
    shard_rows, width = pool.shape
    slots = picks.shape[0] - (experts - 1) * most
    steps = 2
    chunk = width // (2 * steps)
    return pl.pallas_call(
        functools.partial(listed_kernel, experts, most),
        out_shape=[
            jax.ShapeDtypeStruct((experts - 1, most, width // 2), bf16),
            jax.ShapeDtypeStruct((slots, width // 2), bf16),
        ],
        grid_spec=pltpu.PrefetchScalarGridSpec(
            num_scalar_prefetch=1,
            grid=(steps,),
            in_specs=[
                pl.BlockSpec(picks.shape, lambda i, w: (0, 0)),
                pl.BlockSpec((shard_rows, chunk), lambda i, w: (0, (w[1] ^ 1 ^ part) * steps + i)),
            ],
            out_specs=[
                pl.BlockSpec((experts - 1, most, chunk), lambda i, w: (0, 0, i)),
                pl.BlockSpec((slots, chunk), lambda i, w: (0, i)),
            ],
        ),
        compiler_params=pltpu.CompilerParams(vmem_limit_bytes=VMEM_LIMIT),
        cost_estimate=LIGHT,
        name="listed_rows",
    )(where, picks, pool)


def merge_kernel(experts, shard_rows, masks, halves, where_ref, index_ref, own_ref, *refs):
    incoming, sent_refs, block_ref = refs[: experts - 1], refs[experts - 1 : -1], refs[-1]
    me, upper, core = where_ref[0], where_ref[2], where_ref[3]
    most = incoming[0].shape[1]
    block = block_ref.shape[2]
    listed = index_ref[pl.ds(me, 1), :]
    rows = own_ref[...].astype(f32)
    for mask in range(1, experts):
        pick = one_hot(slot_ranks(listed, me ^ mask, shard_rows), most)
        rows = rows + jnp.dot(pick, incoming[mask - 1][0], preferred_element_type=f32)
    rows = rows.astype(bf16)
    for column in range(block_ref.shape[0]):
        block_ref[column] = rows[:, column * block : (column + 1) * block]
    for mask, sent_ref in zip(masks, sent_refs):
        first = ((upper ^ mask) & (halves - 1)) * 4
        for core_mask in range(2):
            for side in range(2):
                sent_ref[core_mask, side] = block_ref[first + 2 * side + (core ^ core_mask)]


def merged_rows(where, index, own, incoming, experts, replicas, shard_rows, masks):
    slots, half = own.shape
    block = 2 * half // replicas
    return pl.pallas_call(
        functools.partial(merge_kernel, experts, shard_rows, masks, replicas // 8),
        out_shape=[jax.ShapeDtypeStruct((2, 2, slots, block), bf16)] * len(masks),
        in_specs=[smem()] + [vmem()] * (experts + 1),
        out_specs=[vmem()] * len(masks),
        scratch_shapes=[pltpu.VMEM((replicas // 2, slots, block), bf16)],
        compiler_params=params(own, own, own, *incoming),
        cost_estimate=LIGHT,
        name="merged_rows",
    )(where, index, own, *incoming)


def forward_kernel(uppers, blocks, where_ref, *refs):
    own, crossed_ref, rest, outs = refs[:uppers], refs[uppers], refs[uppers + 1 :], refs[uppers + 1 + len(blocks.arrays) :]
    side = where_ref[4]
    totals = [jnp.zeros(outs[0].shape, f32) for _ in range(4)]
    for mask in range(uppers):
        peer = crossed_ref.at[mask]
        for side_mask in range(2):
            w = blocks.ref(rest, 4 * mask + 2 * side_mask)
            for rows, first in ((own[mask].at[0], 0), (peer, 2)):
                for matrix in range(2):
                    totals[first + matrix] += jnp.dot(rows[side ^ side_mask], w[matrix], preferred_element_type=f32)
    for out, total in zip(outs, totals):
        out[...] = total


def forward(where, crossed, own, blocks, uppers):
    out = jax.ShapeDtypeStruct((own[0].shape[2], blocks.arrays[0].shape[-1]), f32)
    return pl.pallas_call(
        functools.partial(forward_kernel, uppers, blocks),
        out_shape=[out] * 4,
        in_specs=[smem()] + [vmem()] * (uppers + 1 + len(blocks.arrays)),
        out_specs=[vmem()] * 4,
        compiler_params=params(*own, crossed, *blocks.arrays),
        cost_estimate=LIGHT,
        name="forward_values",
    )(where, *own, crossed, *blocks.arrays)


def delta_kernel(where_ref, count_ref, targets_ref, gate_ref, up_ref, gate_other_ref, up_other_ref, kept_ref, sent_ref):
    side = where_ref[4]
    slots = targets_ref.shape[0]
    gate_value = gate_ref[...] + gate_other_ref[...]
    up_value = up_ref[...] + up_other_ref[...]
    live_count = count_ref[0, 0]
    sigmoid = jax.nn.sigmoid(gate_value)
    activated = gate_value * sigmoid
    silu_slope = sigmoid * (1.0 + gate_value * (1.0 - sigmoid))
    live = (grid_iota((slots, 1), 0) < live_count).astype(f32)
    residual = (activated * up_value - targets_ref[...].astype(f32)) * live / jnp.full((1, 1), live_count, i32).astype(f32)
    gate_delta = (residual * up_value * silu_slope).astype(bf16)
    up_delta = (residual * activated).astype(bf16)
    kept_ref[...] = jnp.where(side == 0, gate_delta, up_delta)
    sent_ref[...] = jnp.where(side == 0, up_delta, gate_delta)


def deltas_of(where, count, targets, values):
    out = jax.ShapeDtypeStruct(targets.shape, bf16)
    return pl.pallas_call(
        delta_kernel,
        out_shape=[out, out],
        in_specs=[smem(), smem()] + [vmem()] * (1 + len(values)),
        out_specs=[vmem()] * 2,
        compiler_params=params(targets, *values),
        cost_estimate=LIGHT,
        name="deltas",
    )(where, count, targets, *values)


def token_contract(left, right):
    return lax.dot_general(left, right, (((0,), (0,)), ((), ())), preferred_element_type=f32)


TILE = 16


class Pieces:
    def __init__(self):
        self.arrays, self.place = [], {}

    def put(self, keys, pieces):
        if isinstance(pieces, list):
            for key, piece in zip(keys, pieces):
                self.place[key] = (len(self.arrays), None)
                self.arrays.append(piece)
            return
        for index, key in enumerate(keys):
            self.place[key] = (len(self.arrays), index)
        self.arrays.append(pieces)

    def ref(self, refs, key):
        array, index = self.place[key]
        return refs[array] if index is None else refs[array].at[index]

    def read(self, refs, key):
        return self.ref(refs, key)[...]


def split_refs(rows, deltas, refs):
    count = len(rows.arrays)
    rest = refs[count:]

    def rows_of(key):
        ref = rows.ref(refs, key)
        return ref.at[0] if len(ref.shape) == 4 else ref

    return rows_of, lambda key: deltas.read(rest, key), rest[len(deltas.arrays) :]


def gram_kernel(replicas, pieces, where_ref, *refs):
    rows, deltas, (gram_ref, table_ref) = split_refs(*pieces, refs)
    me = where_ref[5]
    block = rows(0).shape[2]
    steps = block // TILE
    for mask in range(replicas):
        first = pl.multiple_of((me ^ mask) * TILE, TILE)
        for part in range(2):
            gradient = token_contract(rows(mask)[part], deltas(mask)).astype(bf16)
            for step in range(steps):
                table_ref[part * steps + step, pl.ds(first, TILE), :] = gradient[step * TILE : (step + 1) * TILE]
    size = replicas * TILE
    products = jnp.zeros((size, size), f32)
    for step in range(2 * steps):
        products += lax.dot_general(
            table_ref[step], table_ref[step], (((1,), (1,)), ((), ())), preferred_element_type=f32
        )
    same = (grid_iota((size, size), 0) & (TILE - 1)) == (grid_iota((size, size), 1) & (TILE - 1))
    products = jnp.where(same, products, 0.0)
    down = jnp.concatenate(
        [jnp.sum(products[r * TILE : (r + 1) * TILE], axis=0, keepdims=True) for r in range(replicas)], axis=0
    )
    member = (grid_iota((size, replicas), 0) // TILE == grid_iota((size, replicas), 1)).astype(f32)
    gram_ref[...] = jnp.dot(down, member, preferred_element_type=f32, precision=lax.Precision.HIGHEST)


def gram(where, rows, deltas, replicas):
    depth = 2 * rows.arrays[0].shape[-1]
    hidden = deltas.arrays[0].shape[-1]
    return pl.pallas_call(
        functools.partial(gram_kernel, replicas, (rows, deltas)),
        out_shape=jax.ShapeDtypeStruct((replicas, replicas), f32),
        in_specs=[smem()] + [vmem()] * (len(rows.arrays) + len(deltas.arrays)),
        out_specs=vmem(),
        scratch_shapes=[pltpu.VMEM((depth // TILE, replicas * TILE, hidden), bf16)],
        compiler_params=params(*rows.arrays, *deltas.arrays, jax.ShapeDtypeStruct((replicas * TILE, replicas * TILE), f32)),
        cost_estimate=LIGHT,
        name="gradient_products",
    )(where, *rows.arrays, *deltas.arrays)


def tree_weights(table, replicas):
    down, along = grid_iota((replicas, replicas), 0), grid_iota((replicas, replicas), 1)
    weights = jnp.ones((replicas, 1), f32)
    half = replicas // 2
    while half >= 1:
        same = down == along
        other = ((down + half) & (replicas - 1)) == along
        partner = ((along + half) & (replicas - 1)) == down
        square_down = jnp.sum(jnp.where(same, table, 0.0), axis=1, keepdims=True)
        square_along = jnp.sum(jnp.where(same, table, 0.0), axis=0, keepdims=True)
        inner_down = jnp.sum(jnp.where(other, table, 0.0), axis=1, keepdims=True)
        inner_along = jnp.sum(jnp.where(partner, table, 0.0), axis=0, keepdims=True)
        weight_down = 1.0 - inner_down / (2.0 * square_down + adasum_epsilon)
        weight_along = 1.0 - inner_along / (2.0 * square_along + adasum_epsilon)
        weights = weights * weight_down
        table = weight_down * (table * weight_along)
        table = table + jnp.concatenate([table[half:], table[:half]], axis=0)
        table = table + jnp.concatenate([table[:, half:], table[:, :half]], axis=1)
        half //= 2
    return weights


def combine_kernel(replicas, pieces, where_ref, gram_ref, *refs):
    rows, deltas, (kept_ref, sent_ref, weight_ref) = split_refs(*pieces, refs)
    side, me = where_ref[4], where_ref[5]
    weight_ref[...] = jnp.broadcast_to(tree_weights(gram_ref[...], replicas), weight_ref.shape)
    for ref, part in ((kept_ref, side), (sent_ref, 1 - side)):
        total = jnp.zeros(ref.shape, f32)
        for mask in range(replicas):
            gradient = token_contract(rows(mask)[part], deltas(mask))
            total = total + weight_ref[pl.ds(me ^ mask, 1), 0:1] * gradient
        ref[...] = total


def combine(where, products, rows, deltas):
    replicas = products.shape[0]
    out = jax.ShapeDtypeStruct((rows.arrays[0].shape[-1], deltas.arrays[0].shape[-1]), f32)
    return pl.pallas_call(
        functools.partial(combine_kernel, replicas, (rows, deltas)),
        out_shape=[out, out],
        in_specs=[smem(), vmem()] + [vmem()] * (len(rows.arrays) + len(deltas.arrays)),
        out_specs=[vmem()] * 2,
        scratch_shapes=[pltpu.VMEM((replicas, 128), f32)],
        compiler_params=params(*rows.arrays, *deltas.arrays),
        cost_estimate=LIGHT,
        name="combined_gradient",
    )(where, products, *rows.arrays, *deltas.arrays)


def shards(pool, row_index, counts, targets, weights, first_moment, second_moment):
    replicas = lax.axis_size("replica")
    experts = lax.axis_size("expert")
    uppers = replicas // 4
    position = lax.axis_index("replica")
    expert_position = lax.axis_index("expert")
    core, side, upper = position & 1, position >> 1 & 1, position >> 2
    where = jnp.stack([expert_position, position // (replicas // 2), upper, core, side, position]).astype(i32)
    index = row_index[:, 0, :]
    local_pool = pool[0]
    shard_rows = local_pool.shape[0]
    most = 3 * index.shape[1] // (2 * experts)

    halves = uppers // 2
    upper_masks = [4 << bit for bit in range(uppers.bit_length() - 1)]
    picks = picks_of(where, index, experts, most, shard_rows)
    far, near = list(range(halves, uppers)), list(range(halves))
    packed = [None] * uppers
    for part, masks in enumerate((far, near)):
        outgoing, own = listed_rows(where, picks, local_pool, experts, most, part)
        incoming = [swapped(outgoing[mask - 1 : mask], "expert", mask) for mask in range(1, experts)]
        if part == 0:
            lowered = weights[0].astype(bf16)
            by_upper = gathered(lowered, upper_masks)
            by_upper = [by_upper[4 * mask] for mask in range(uppers)]
            own, picks, *_ = lax.optimization_barrier((own, picks, by_upper[halves], by_upper[1]))
            blocks = Pieces()
            blocks.put([4 * mask for mask in range(uppers)], by_upper)
            besides = []
            for group in (near, far):
                besides.append(swapped(jnp.stack([by_upper[mask] for mask in group]), "replica", SIDE))
                blocks.put([4 * mask | SIDE for mask in group], besides[-1])
        else:
            own, _ = lax.optimization_barrier((own, besides[0]))
        packed[masks[0] : masks[-1] + 1] = merged_rows(
            where, index, own, incoming, experts, replicas, shard_rows, masks
        )

    crossed = swapped(jnp.stack([piece[1] for piece in packed]), "replica", CORE)
    values = forward(where, crossed, packed, blocks, uppers)

    rows = Pieces()
    rows.put([0], [packed[0]])
    others_of = far + near[1:]
    arrived = [swapped(packed[mask], "replica", 4 * mask) for mask in others_of]
    other = swapped(jnp.stack([piece[1] for piece in arrived]), "replica", CORE)
    for mask, piece in zip(others_of, arrived):
        rows.put([4 * mask], [piece])
    rows.put([4 * mask | CORE for mask in others_of], other)
    rows.put([CORE], crossed)
    values = list(values[:2]) + [swapped(value, "replica", CORE) for value in values[2:]]
    kept_delta, sent_delta = deltas_of(where, counts, targets[0, 0], values)
    side_deltas = [kept_delta, swapped(sent_delta, "replica", SIDE)]

    deltas = Pieces()
    far_mask, near_masks = upper_masks[-1], upper_masks[:-1]

    def hold(keys, pieces):
        both = jnp.stack(pieces)
        deltas.put(keys, both)
        across = swapped(both, "replica", CORE)
        deltas.put([key | CORE for key in keys], across)
        return both, across

    hold([0, SIDE], side_deltas)
    kept_far = swapped(kept_delta, "replica", far_mask)
    kept_near, beside_near = [gathered(piece, near_masks) for piece in side_deltas]
    keys = [mask for mask in kept_near if mask > 0]
    kept_near, beside_near = [kept_near[key] for key in keys], [beside_near[key] for key in keys]
    beside_own, *_ = lax.optimization_barrier((side_deltas[1], *kept_near))
    beside_far = swapped(beside_own, "replica", far_mask)
    all_here = [packed[0][0]] + [piece[0] for piece in arrived] + [crossed[0]] + [other[i] for i in range(len(arrived))]
    all_here, _ = lax.optimization_barrier((jnp.stack(all_here), side_deltas[1]))
    keys_beside = [4 * mask | SIDE for mask in [0] + others_of]
    rows.put(keys_beside + [key | CORE for key in keys_beside], swapped(all_here, "replica", SIDE))
    hold(keys + [key | SIDE for key in keys], kept_near + beside_near)
    far, _ = hold([far_mask, far_mask | SIDE], [kept_far, beside_far])
    far, *_ = lax.optimization_barrier((far, *kept_near, *beside_near))
    for key, piece in gathered(far, near_masks).items():
        if key > 0:
            keys = [far_mask | key, far_mask | key | SIDE]
            deltas.put(keys, piece)
            deltas.put([key | CORE for key in keys], swapped(piece, "replica", CORE))

    products = gram(where, rows, deltas, replicas)
    products = products + swapped(products, "replica", CORE)
    mask = 4
    while mask < replicas:
        products = products + swapped(products, "replica", mask)
        mask *= 2
    kept_block, sent_block = combine(where, products, rows, deltas)
    other_block = swapped(sent_block.astype(bf16), "replica", SIDE).astype(f32)
    combined = jnp.where(
        side == 0, jnp.stack([kept_block, other_block]), jnp.stack([other_block, kept_block])
    )
    new_weight, moment_one, moment_two = adam_update(
        combined, weights[0], first_moment[0], second_moment[0]
    )
    return (new_weight[None], moment_one[None], moment_two[None])


def solution(mesh):
    in_specs = (
        P("replica", "expert", None),
        P(None, "replica", None),
        P("expert", "replica"),
        P("expert", "replica", None, None),
        P("expert", None, "replica", None),
        P("expert", None, "replica", None),
        P("expert", None, "replica", None),
    )
    out_specs = (
        P("expert", None, "replica", None),
        P("expert", None, "replica", None),
        P("expert", None, "replica", None),
    )
    return jax.shard_map(shards, mesh=mesh, in_specs=in_specs, out_specs=out_specs, check_vma=False)
```

```python
import functools
import math

import jax
import jax.numpy as jnp
from jax import lax
from jax.experimental import pallas as pl
from jax.experimental.pallas import tpu as pltpu
from jax.sharding import PartitionSpec as P

STEP = 3


beta_first = 0.9
beta_second = 0.999
learning_rate = 0.02
decay_rate = 0.1
adam_epsilon = 1e-08
adasum_epsilon = 1e-12

CORE, SIDE = 1, 2
VMEM_LIMIT = 50 * 1024 * 1024
LIGHT = pl.CostEstimate(flops=1, bytes_accessed=1, transcendentals=0)
f32, bf16, i32 = jnp.float32, jnp.bfloat16, jnp.int32


def gathered(x, masks):
    pieces = {0: x}
    for mask in reversed(masks):
        pieces.update({mask | held: swapped(piece, "replica", mask) for held, piece in list(pieces.items())})
    return pieces


def swapped(x, axis, mask):
    return lax.ppermute(x, axis, [(i, i ^ mask) for i in range(lax.axis_size(axis))])


def vmem():
    return pl.BlockSpec(memory_space=pltpu.VMEM)


def smem():
    return pl.BlockSpec(memory_space=pltpu.SMEM)


def params(*arrays):
    total = 0
    for array in arrays:
        *lead, rows, columns = array.shape
        total += math.prod(lead) * -(-rows // 16) * 16 * -(-columns // 128) * 128 * array.dtype.itemsize
    return pltpu.CompilerParams(vmem_limit_bytes=min(2 * total + 4 * 1024 * 1024, VMEM_LIMIT))


def adam_update(gradient, weight, moment_one, moment_two):
    moment_one = beta_first * moment_one + (1.0 - beta_first) * gradient
    moment_two = beta_second * moment_two + (1.0 - beta_second) * gradient * gradient
    first_hat = moment_one / (1.0 - beta_first**STEP)
    second_hat = moment_two / (1.0 - beta_second**STEP)
    weight = weight - learning_rate * (
        first_hat / (jnp.sqrt(second_hat) + adam_epsilon) + decay_rate * weight
    )
    return (weight, moment_one, moment_two)


def grid_iota(shape, dim):
    return lax.broadcasted_iota(i32, shape, dim)


def compacted_rows(listed, block, shard_rows, most):
    slots = listed.shape[1]
    local = listed - block * shard_rows
    held = (local >= 0) & (local < shard_rows)
    down, along = grid_iota((slots, slots), 0), grid_iota((slots, slots), 1)
    held_wide = jnp.broadcast_to(held.astype(i32), (slots, slots))
    held_column = jnp.sum(jnp.where(down == along, held_wide, 0), axis=1, keepdims=True)
    rank = jnp.sum(jnp.where(down < along, jnp.broadcast_to(held_column, (slots, slots)), 0), axis=0, keepdims=True)
    place = jnp.where(held, rank, -1)
    hit = grid_iota((most, slots), 0) == jnp.broadcast_to(place, (most, slots))
    return jnp.sum(jnp.where(hit, jnp.broadcast_to(local + 1, (most, slots)), 0), axis=1, keepdims=True) - 1


def slot_rows(listed, block, shard_rows):
    slots = listed.shape[1]
    local = listed - block * shard_rows
    held = (local >= 0) & (local < shard_rows)
    value = jnp.where(held, local + 1, 0)
    diagonal = grid_iota((slots, slots), 0) == grid_iota((slots, slots), 1)
    return jnp.sum(jnp.where(diagonal, jnp.broadcast_to(value, (slots, slots)), 0), axis=1, keepdims=True) - 1


def slot_ranks(listed, block, shard_rows):
    slots = listed.shape[1]
    local = listed - block * shard_rows
    held = ((local >= 0) & (local < shard_rows)).astype(i32)
    held_wide = jnp.broadcast_to(held, (slots, slots))
    down, along = grid_iota((slots, slots), 0), grid_iota((slots, slots), 1)
    rank = jnp.sum(jnp.where(along < down, held_wide, 0), axis=1, keepdims=True)
    own = jnp.sum(jnp.where(along == down, held_wide, 0), axis=1, keepdims=True)
    return jnp.where(own > 0, rank, -1)


def one_hot(column, width):
    return (grid_iota((column.shape[0], width), 1) == column).astype(f32).astype(bf16)


def pick_kernel(experts, most, shard_rows, where_ref, index_ref, pick_ref):
    slots = index_ref.shape[1]
    me = where_ref[0]
    pick_ref[:slots] = one_hot(slot_rows(index_ref[pl.ds(me, 1), :], me, shard_rows), shard_rows)
    for mask in range(1, experts):
        listed = index_ref[pl.ds(me ^ mask, 1), :]
        first = slots + (mask - 1) * most
        pick_ref[first : first + most] = one_hot(compacted_rows(listed, me, shard_rows, most), shard_rows)


def picks_of(where, index, experts, most, shard_rows):
    return pl.pallas_call(
        functools.partial(pick_kernel, experts, most, shard_rows),
        out_shape=jax.ShapeDtypeStruct((index.shape[1] + (experts - 1) * most, shard_rows), bf16),
        in_specs=[smem(), vmem()],
        out_specs=vmem(),
        compiler_params=params(jax.ShapeDtypeStruct((2 * most, shard_rows), f32)),
        cost_estimate=LIGHT,
        name="row_picks",
    )(where, index)


def listed_kernel(experts, most, where_ref, pick_ref, pool_ref, out_ref, own_ref):
    slots = own_ref.shape[0]
    rows = jnp.dot(pick_ref[...], pool_ref[...], preferred_element_type=f32).astype(bf16)
    own_ref[...] = rows[:slots]
    for mask in range(1, experts):
        out_ref[mask - 1] = rows[slots + (mask - 1) * most : slots + mask * most]


def listed_rows(where, picks, pool, experts, most, part):
    shard_rows, width = pool.shape
    slots = picks.shape[0] - (experts - 1) * most
    steps = 2
    chunk = width // (2 * steps)
    return pl.pallas_call(
        functools.partial(listed_kernel, experts, most),
        out_shape=[
            jax.ShapeDtypeStruct((experts - 1, most, width // 2), bf16),
            jax.ShapeDtypeStruct((slots, width // 2), bf16),
        ],
        grid_spec=pltpu.PrefetchScalarGridSpec(
            num_scalar_prefetch=1,
            grid=(steps,),
            in_specs=[
                pl.BlockSpec(picks.shape, lambda i, w: (0, 0)),
                pl.BlockSpec((shard_rows, chunk), lambda i, w: (0, (w[1] ^ 1 ^ part) * steps + i)),
            ],
            out_specs=[
                pl.BlockSpec((experts - 1, most, chunk), lambda i, w: (0, 0, i)),
                pl.BlockSpec((slots, chunk), lambda i, w: (0, i)),
            ],
        ),
        compiler_params=pltpu.CompilerParams(vmem_limit_bytes=VMEM_LIMIT),
        cost_estimate=LIGHT,
        name="listed_rows",
    )(where, picks, pool)


def merge_kernel(experts, shard_rows, masks, halves, where_ref, index_ref, own_ref, *refs):
    incoming, sent_refs, block_ref = refs[: experts - 1], refs[experts - 1 : -1], refs[-1]
    me, upper, core = where_ref[0], where_ref[2], where_ref[3]
    most = incoming[0].shape[1]
    block = block_ref.shape[2]
    listed = index_ref[pl.ds(me, 1), :]
    rows = own_ref[...].astype(f32)
    for mask in range(1, experts):
        pick = one_hot(slot_ranks(listed, me ^ mask, shard_rows), most)
        rows = rows + jnp.dot(pick, incoming[mask - 1][0], preferred_element_type=f32)
    rows = rows.astype(bf16)
    for column in range(block_ref.shape[0]):
        block_ref[column] = rows[:, column * block : (column + 1) * block]
    for mask, sent_ref in zip(masks, sent_refs):
        first = ((upper ^ mask) & (halves - 1)) * 4
        for core_mask in range(2):
            for side in range(2):
                sent_ref[core_mask, side] = block_ref[first + 2 * side + (core ^ core_mask)]


def merged_rows(where, index, own, incoming, experts, replicas, shard_rows, masks):
    slots, half = own.shape
    block = 2 * half // replicas
    return pl.pallas_call(
        functools.partial(merge_kernel, experts, shard_rows, masks, replicas // 8),
        out_shape=[jax.ShapeDtypeStruct((2, 2, slots, block), bf16)] * len(masks),
        in_specs=[smem()] + [vmem()] * (experts + 1),
        out_specs=[vmem()] * len(masks),
        scratch_shapes=[pltpu.VMEM((replicas // 2, slots, block), bf16)],
        compiler_params=params(own, own, own, *incoming),
        cost_estimate=LIGHT,
        name="merged_rows",
    )(where, index, own, *incoming)


def forward_kernel(uppers, blocks, where_ref, *refs):
    own, crossed_ref, rest, outs = refs[:uppers], refs[uppers], refs[uppers + 1 :], refs[uppers + 1 + len(blocks.arrays) :]
    side = where_ref[4]
    totals = [jnp.zeros(outs[0].shape, f32) for _ in range(4)]
    for mask in range(uppers):
        peer = crossed_ref.at[mask]
        for side_mask in range(2):
            w = blocks.ref(rest, 4 * mask + 2 * side_mask)
            for rows, first in ((own[mask].at[0], 0), (peer, 2)):
                for matrix in range(2):
                    totals[first + matrix] += jnp.dot(rows[side ^ side_mask], w[matrix], preferred_element_type=f32)
    for out, total in zip(outs, totals):
        out[...] = total


def forward(where, crossed, own, blocks, uppers):
    out = jax.ShapeDtypeStruct((own[0].shape[2], blocks.arrays[0].shape[-1]), f32)
    return pl.pallas_call(
        functools.partial(forward_kernel, uppers, blocks),
        out_shape=[out] * 4,
        in_specs=[smem()] + [vmem()] * (uppers + 1 + len(blocks.arrays)),
        out_specs=[vmem()] * 4,
        compiler_params=params(*own, crossed, *blocks.arrays),
        cost_estimate=LIGHT,
        name="forward_values",
    )(where, *own, crossed, *blocks.arrays)


def delta_kernel(where_ref, count_ref, targets_ref, gate_ref, up_ref, gate_other_ref, up_other_ref, kept_ref, sent_ref):
    side = where_ref[4]
    slots = targets_ref.shape[0]
    gate_value = gate_ref[...] + gate_other_ref[...]
    up_value = up_ref[...] + up_other_ref[...]
    live_count = count_ref[0, 0]
    sigmoid = jax.nn.sigmoid(gate_value)
    activated = gate_value * sigmoid
    silu_slope = sigmoid * (1.0 + gate_value * (1.0 - sigmoid))
    live = (grid_iota((slots, 1), 0) < live_count).astype(f32)
    residual = (activated * up_value - targets_ref[...].astype(f32)) * live / jnp.full((1, 1), live_count, i32).astype(f32)
    gate_delta = (residual * up_value * silu_slope).astype(bf16)
    up_delta = (residual * activated).astype(bf16)
    kept_ref[...] = jnp.where(side == 0, gate_delta, up_delta)
    sent_ref[...] = jnp.where(side == 0, up_delta, gate_delta)


def deltas_of(where, count, targets, values):
    out = jax.ShapeDtypeStruct(targets.shape, bf16)
    return pl.pallas_call(
        delta_kernel,
        out_shape=[out, out],
        in_specs=[smem(), smem()] + [vmem()] * (1 + len(values)),
        out_specs=[vmem()] * 2,
        compiler_params=params(targets, *values),
        cost_estimate=LIGHT,
        name="deltas",
    )(where, count, targets, *values)


def token_contract(left, right):
    return lax.dot_general(left, right, (((0,), (0,)), ((), ())), preferred_element_type=f32)


TILE = 16


class Pieces:
    def __init__(self):
        self.arrays, self.place = [], {}

    def put(self, keys, pieces):
        if isinstance(pieces, list):
            for key, piece in zip(keys, pieces):
                self.place[key] = (len(self.arrays), None)
                self.arrays.append(piece)
            return
        for index, key in enumerate(keys):
            self.place[key] = (len(self.arrays), index)
        self.arrays.append(pieces)

    def ref(self, refs, key):
        array, index = self.place[key]
        return refs[array] if index is None else refs[array].at[index]

    def read(self, refs, key):
        return self.ref(refs, key)[...]


def split_refs(rows, deltas, refs):
    count = len(rows.arrays)
    rest = refs[count:]

    def rows_of(key):
        ref = rows.ref(refs, key)
        return ref.at[0] if len(ref.shape) == 4 else ref

    return rows_of, lambda key: deltas.read(rest, key), rest[len(deltas.arrays) :]


def gram_kernel(replicas, pieces, where_ref, *refs):
    rows, deltas, (gram_ref, table_ref) = split_refs(*pieces, refs)
    me = where_ref[5]
    block = rows(0).shape[2]
    steps = block // TILE
    for mask in range(replicas):
        first = pl.multiple_of((me ^ mask) * TILE, TILE)
        for part in range(2):
            gradient = token_contract(rows(mask)[part], deltas(mask)).astype(bf16)
            for step in range(steps):
                table_ref[part * steps + step, pl.ds(first, TILE), :] = gradient[step * TILE : (step + 1) * TILE]
    size = replicas * TILE
    products = jnp.zeros((size, size), f32)
    for step in range(2 * steps):
        products += lax.dot_general(
            table_ref[step], table_ref[step], (((1,), (1,)), ((), ())), preferred_element_type=f32
        )
    same = (grid_iota((size, size), 0) & (TILE - 1)) == (grid_iota((size, size), 1) & (TILE - 1))
    products = jnp.where(same, products, 0.0)
    down = jnp.concatenate(
        [jnp.sum(products[r * TILE : (r + 1) * TILE], axis=0, keepdims=True) for r in range(replicas)], axis=0
    )
    member = (grid_iota((size, replicas), 0) // TILE == grid_iota((size, replicas), 1)).astype(f32)
    gram_ref[...] = jnp.dot(down, member, preferred_element_type=f32, precision=lax.Precision.HIGHEST)


def gram(where, rows, deltas, replicas):
    depth = 2 * rows.arrays[0].shape[-1]
    hidden = deltas.arrays[0].shape[-1]
    return pl.pallas_call(
        functools.partial(gram_kernel, replicas, (rows, deltas)),
        out_shape=jax.ShapeDtypeStruct((replicas, replicas), f32),
        in_specs=[smem()] + [vmem()] * (len(rows.arrays) + len(deltas.arrays)),
        out_specs=vmem(),
        scratch_shapes=[pltpu.VMEM((depth // TILE, replicas * TILE, hidden), bf16)],
        compiler_params=params(*rows.arrays, *deltas.arrays, jax.ShapeDtypeStruct((replicas * TILE, replicas * TILE), f32)),
        cost_estimate=LIGHT,
        name="gradient_products",
    )(where, *rows.arrays, *deltas.arrays)


def tree_weights(table, replicas):
    down, along = grid_iota((replicas, replicas), 0), grid_iota((replicas, replicas), 1)
    weights = jnp.ones((replicas, 1), f32)
    half = replicas // 2
    while half >= 1:
        same = down == along
        other = ((down + half) & (replicas - 1)) == along
        partner = ((along + half) & (replicas - 1)) == down
        square_down = jnp.sum(jnp.where(same, table, 0.0), axis=1, keepdims=True)
        square_along = jnp.sum(jnp.where(same, table, 0.0), axis=0, keepdims=True)
        inner_down = jnp.sum(jnp.where(other, table, 0.0), axis=1, keepdims=True)
        inner_along = jnp.sum(jnp.where(partner, table, 0.0), axis=0, keepdims=True)
        weight_down = 1.0 - inner_down / (2.0 * square_down + adasum_epsilon)
        weight_along = 1.0 - inner_along / (2.0 * square_along + adasum_epsilon)
        weights = weights * weight_down
        table = weight_down * (table * weight_along)
        table = table + jnp.concatenate([table[half:], table[:half]], axis=0)
        table = table + jnp.concatenate([table[:, half:], table[:, :half]], axis=1)
        half //= 2
    return weights


def combine_kernel(replicas, pieces, where_ref, gram_ref, *refs):
    rows, deltas, (kept_ref, sent_ref, weight_ref) = split_refs(*pieces, refs)
    side, me = where_ref[4], where_ref[5]
    weight_ref[...] = jnp.broadcast_to(tree_weights(gram_ref[...], replicas), weight_ref.shape)
    for ref, part in ((kept_ref, side), (sent_ref, 1 - side)):
        total = jnp.zeros(ref.shape, f32)
        for mask in range(replicas):
            gradient = token_contract(rows(mask)[part], deltas(mask))
            total = total + weight_ref[pl.ds(me ^ mask, 1), 0:1] * gradient
        ref[...] = total


def combine(where, products, rows, deltas):
    replicas = products.shape[0]
    out = jax.ShapeDtypeStruct((rows.arrays[0].shape[-1], deltas.arrays[0].shape[-1]), f32)
    return pl.pallas_call(
        functools.partial(combine_kernel, replicas, (rows, deltas)),
        out_shape=[out, out],
        in_specs=[smem(), vmem()] + [vmem()] * (len(rows.arrays) + len(deltas.arrays)),
        out_specs=[vmem()] * 2,
        scratch_shapes=[pltpu.VMEM((replicas, 128), f32)],
        compiler_params=params(*rows.arrays, *deltas.arrays),
        cost_estimate=LIGHT,
        name="combined_gradient",
    )(where, products, *rows.arrays, *deltas.arrays)


def shards(pool, row_index, counts, targets, weights, first_moment, second_moment):
    replicas = lax.axis_size("replica")
    experts = lax.axis_size("expert")
    uppers = replicas // 4
    position = lax.axis_index("replica")
    expert_position = lax.axis_index("expert")
    core, side, upper = position & 1, position >> 1 & 1, position >> 2
    where = jnp.stack([expert_position, position // (replicas // 2), upper, core, side, position]).astype(i32)
    index = row_index[:, 0, :]
    local_pool = pool[0]
    shard_rows = local_pool.shape[0]
    most = 3 * index.shape[1] // (2 * experts)

    halves = uppers // 2
    upper_masks = [4 << bit for bit in range(uppers.bit_length() - 1)]
    picks = picks_of(where, index, experts, most, shard_rows)
    far, near = list(range(halves, uppers)), list(range(halves))
    packed = [None] * uppers
    for part, masks in enumerate((far, near)):
        outgoing, own = listed_rows(where, picks, local_pool, experts, most, part)
        incoming = [swapped(outgoing[mask - 1 : mask], "expert", mask) for mask in range(1, experts)]
        if part == 0:
            lowered = weights[0].astype(bf16)
            by_upper = gathered(lowered, upper_masks)
            by_upper = [by_upper[4 * mask] for mask in range(uppers)]
            own, picks, *_ = lax.optimization_barrier((own, picks, by_upper[halves], by_upper[1]))
            blocks = Pieces()
            blocks.put([4 * mask for mask in range(uppers)], by_upper)
            besides = []
            for group in (near, far):
                besides.append(swapped(jnp.stack([by_upper[mask] for mask in group]), "replica", SIDE))
                blocks.put([4 * mask | SIDE for mask in group], besides[-1])
        else:
            own, _ = lax.optimization_barrier((own, besides[0]))
        packed[masks[0] : masks[-1] + 1] = merged_rows(
            where, index, own, incoming, experts, replicas, shard_rows, masks
        )

    crossed = swapped(jnp.stack([piece[1] for piece in packed]), "replica", CORE)
    values = forward(where, crossed, packed, blocks, uppers)

    rows = Pieces()
    rows.put([0], [packed[0]])
    others_of = far + near[1:]
    arrived = [swapped(packed[mask], "replica", 4 * mask) for mask in others_of]
    other = swapped(jnp.stack([piece[1] for piece in arrived]), "replica", CORE)
    for mask, piece in zip(others_of, arrived):
        rows.put([4 * mask], [piece])
    rows.put([4 * mask | CORE for mask in others_of], other)
    rows.put([CORE], crossed)
    values = list(values[:2]) + [swapped(value, "replica", CORE) for value in values[2:]]
    kept_delta, sent_delta = deltas_of(where, counts, targets[0, 0], values)
    side_deltas = [kept_delta, swapped(sent_delta, "replica", SIDE)]

    deltas = Pieces()
    far_mask, near_masks = upper_masks[-1], upper_masks[:-1]

    def hold(keys, pieces):
        both = jnp.stack(pieces)
        deltas.put(keys, both)
        across = swapped(both, "replica", CORE)
        deltas.put([key | CORE for key in keys], across)
        return both, across

    hold([0, SIDE], side_deltas)
    kept_far = swapped(kept_delta, "replica", far_mask)
    kept_near, beside_near = [gathered(piece, near_masks) for piece in side_deltas]
    keys = [mask for mask in kept_near if mask > 0]
    kept_near, beside_near = [kept_near[key] for key in keys], [beside_near[key] for key in keys]
    beside_own, *_ = lax.optimization_barrier((side_deltas[1], *kept_near))
    beside_far = swapped(beside_own, "replica", far_mask)
    all_here = [packed[0][0]] + [piece[0] for piece in arrived] + [crossed[0]] + [other[i] for i in range(len(arrived))]
    all_here, _ = lax.optimization_barrier((jnp.stack(all_here), side_deltas[1]))
    keys_beside = [4 * mask | SIDE for mask in [0] + others_of]
    rows.put(keys_beside + [key | CORE for key in keys_beside], swapped(all_here, "replica", SIDE))
    hold(keys + [key | SIDE for key in keys], kept_near + beside_near)
    far, _ = hold([far_mask, far_mask | SIDE], [kept_far, beside_far])
    far, *_ = lax.optimization_barrier((far, *kept_near, *beside_near))
    for key, piece in gathered(far, near_masks).items():
        if key > 0:
            keys = [far_mask | key, far_mask | key | SIDE]
            deltas.put(keys, piece)
            deltas.put([key | CORE for key in keys], swapped(piece, "replica", CORE))

    products = gram(where, rows, deltas, replicas)
    products = products + swapped(products, "replica", CORE)
    mask = 4
    while mask < replicas:
        products = products + swapped(products, "replica", mask)
        mask *= 2
    kept_block, sent_block = combine(where, products, rows, deltas)
    other_block = swapped(sent_block, "replica", SIDE)
    combined = jnp.where(
        side == 0, jnp.stack([kept_block, other_block]), jnp.stack([other_block, kept_block])
    )
    new_weight, moment_one, moment_two = adam_update(
        combined, weights[0], first_moment[0], second_moment[0]
    )
    return (new_weight[None], moment_one[None], moment_two[None])


def solution(mesh):
    in_specs = (
        P("replica", "expert", None),
        P(None, "replica", None),
        P("expert", "replica"),
        P("expert", "replica", None, None),
        P("expert", None, "replica", None),
        P("expert", None, "replica", None),
        P("expert", None, "replica", None),
    )
    out_specs = (
        P("expert", None, "replica", None),
        P("expert", None, "replica", None),
        P("expert", None, "replica", None),
    )
    return jax.shard_map(shards, mesh=mesh, in_specs=in_specs, out_specs=out_specs, check_vma=False)
```

```python
import functools
import math

import jax
import jax.numpy as jnp
from jax import lax
from jax.experimental import pallas as pl
from jax.experimental.pallas import tpu as pltpu
from jax.sharding import PartitionSpec as P

STEP = 3


beta_first = 0.9
beta_second = 0.999
learning_rate = 0.02
decay_rate = 0.1
adam_epsilon = 1e-08
adasum_epsilon = 1e-12

CORE, SIDE = 1, 2
VMEM_LIMIT = 50 * 1024 * 1024
LIGHT = pl.CostEstimate(flops=1, bytes_accessed=1, transcendentals=0)
f32, bf16, i32 = jnp.float32, jnp.bfloat16, jnp.int32


def gathered(x, masks):
    pieces = {0: x}
    for mask in reversed(masks):
        pieces.update({mask | held: swapped(piece, "replica", mask) for held, piece in list(pieces.items())})
    return pieces


def swapped(x, axis, mask):
    return lax.ppermute(x, axis, [(i, i ^ mask) for i in range(lax.axis_size(axis))])


def vmem():
    return pl.BlockSpec(memory_space=pltpu.VMEM)


def smem():
    return pl.BlockSpec(memory_space=pltpu.SMEM)


def params(*arrays):
    total = 0
    for array in arrays:
        *lead, rows, columns = array.shape
        total += math.prod(lead) * -(-rows // 16) * 16 * -(-columns // 128) * 128 * array.dtype.itemsize
    return pltpu.CompilerParams(vmem_limit_bytes=min(2 * total + 4 * 1024 * 1024, VMEM_LIMIT))


def adam_update(gradient, weight, moment_one, moment_two):
    moment_one = beta_first * moment_one + (1.0 - beta_first) * gradient
    moment_two = beta_second * moment_two + (1.0 - beta_second) * gradient * gradient
    first_hat = moment_one / (1.0 - beta_first**STEP)
    second_hat = moment_two / (1.0 - beta_second**STEP)
    weight = weight - learning_rate * (
        first_hat / (jnp.sqrt(second_hat) + adam_epsilon) + decay_rate * weight
    )
    return (weight, moment_one, moment_two)


def grid_iota(shape, dim):
    return lax.broadcasted_iota(i32, shape, dim)


def compacted_rows(listed, block, shard_rows, most):
    slots = listed.shape[1]
    local = listed - block * shard_rows
    held = (local >= 0) & (local < shard_rows)
    down, along = grid_iota((slots, slots), 0), grid_iota((slots, slots), 1)
    held_wide = jnp.broadcast_to(held.astype(i32), (slots, slots))
    held_column = jnp.sum(jnp.where(down == along, held_wide, 0), axis=1, keepdims=True)
    rank = jnp.sum(jnp.where(down < along, jnp.broadcast_to(held_column, (slots, slots)), 0), axis=0, keepdims=True)
    place = jnp.where(held, rank, -1)
    hit = grid_iota((most, slots), 0) == jnp.broadcast_to(place, (most, slots))
    return jnp.sum(jnp.where(hit, jnp.broadcast_to(local + 1, (most, slots)), 0), axis=1, keepdims=True) - 1


def slot_rows(listed, block, shard_rows):
    slots = listed.shape[1]
    local = listed - block * shard_rows
    held = (local >= 0) & (local < shard_rows)
    value = jnp.where(held, local + 1, 0)
    diagonal = grid_iota((slots, slots), 0) == grid_iota((slots, slots), 1)
    return jnp.sum(jnp.where(diagonal, jnp.broadcast_to(value, (slots, slots)), 0), axis=1, keepdims=True) - 1


def slot_ranks(listed, block, shard_rows):
    slots = listed.shape[1]
    local = listed - block * shard_rows
    held = ((local >= 0) & (local < shard_rows)).astype(i32)
    held_wide = jnp.broadcast_to(held, (slots, slots))
    down, along = grid_iota((slots, slots), 0), grid_iota((slots, slots), 1)
    rank = jnp.sum(jnp.where(along < down, held_wide, 0), axis=1, keepdims=True)
    own = jnp.sum(jnp.where(along == down, held_wide, 0), axis=1, keepdims=True)
    return jnp.where(own > 0, rank, -1)


def one_hot(column, width):
    return (grid_iota((column.shape[0], width), 1) == column).astype(f32).astype(bf16)


def pick_kernel(experts, most, shard_rows, where_ref, index_ref, pick_ref):
    slots = index_ref.shape[1]
    me = where_ref[0]
    pick_ref[:slots] = one_hot(slot_rows(index_ref[pl.ds(me, 1), :], me, shard_rows), shard_rows)
    for mask in range(1, experts):
        listed = index_ref[pl.ds(me ^ mask, 1), :]
        first = slots + (mask - 1) * most
        pick_ref[first : first + most] = one_hot(compacted_rows(listed, me, shard_rows, most), shard_rows)


def picks_of(where, index, experts, most, shard_rows):
    return pl.pallas_call(
        functools.partial(pick_kernel, experts, most, shard_rows),
        out_shape=jax.ShapeDtypeStruct((index.shape[1] + (experts - 1) * most, shard_rows), bf16),
        in_specs=[smem(), vmem()],
        out_specs=vmem(),
        compiler_params=params(jax.ShapeDtypeStruct((2 * most, shard_rows), f32)),
        cost_estimate=LIGHT,
        name="row_picks",
    )(where, index)


def listed_kernel(experts, most, where_ref, pick_ref, pool_ref, out_ref, own_ref):
    slots = own_ref.shape[0]
    rows = jnp.dot(pick_ref[...], pool_ref[...], preferred_element_type=f32).astype(bf16)
    own_ref[...] = rows[:slots]
    for mask in range(1, experts):
        out_ref[mask - 1] = rows[slots + (mask - 1) * most : slots + mask * most]


def listed_rows(where, picks, pool, experts, most, part):
    shard_rows, width = pool.shape
    slots = picks.shape[0] - (experts - 1) * most
    steps = 2
    chunk = width // (2 * steps)
    return pl.pallas_call(
        functools.partial(listed_kernel, experts, most),
        out_shape=[
            jax.ShapeDtypeStruct((experts - 1, most, width // 2), bf16),
            jax.ShapeDtypeStruct((slots, width // 2), bf16),
        ],
        grid_spec=pltpu.PrefetchScalarGridSpec(
            num_scalar_prefetch=1,
            grid=(steps,),
            in_specs=[
                pl.BlockSpec(picks.shape, lambda i, w: (0, 0)),
                pl.BlockSpec((shard_rows, chunk), lambda i, w: (0, (w[1] ^ 1 ^ part) * steps + i)),
            ],
            out_specs=[
                pl.BlockSpec((experts - 1, most, chunk), lambda i, w: (0, 0, i)),
                pl.BlockSpec((slots, chunk), lambda i, w: (0, i)),
            ],
        ),
        compiler_params=pltpu.CompilerParams(vmem_limit_bytes=VMEM_LIMIT),
        cost_estimate=LIGHT,
        name="listed_rows",
    )(where, picks, pool)


def merge_kernel(experts, shard_rows, masks, halves, where_ref, index_ref, own_ref, *refs):
    incoming, sent_refs, block_ref = refs[: experts - 1], refs[experts - 1 : -1], refs[-1]
    me, upper, core = where_ref[0], where_ref[2], where_ref[3]
    most = incoming[0].shape[1]
    block = block_ref.shape[2]
    listed = index_ref[pl.ds(me, 1), :]
    rows = own_ref[...].astype(f32)
    for mask in range(1, experts):
        pick = one_hot(slot_ranks(listed, me ^ mask, shard_rows), most)
        rows = rows + jnp.dot(pick, incoming[mask - 1][0], preferred_element_type=f32)
    rows = rows.astype(bf16)
    for column in range(block_ref.shape[0]):
        block_ref[column] = rows[:, column * block : (column + 1) * block]
    for mask, sent_ref in zip(masks, sent_refs):
        first = ((upper ^ mask) & (halves - 1)) * 4
        for core_mask in range(2):
            for side in range(2):
                sent_ref[core_mask, side] = block_ref[first + 2 * side + (core ^ core_mask)]


def merged_rows(where, index, own, incoming, experts, replicas, shard_rows, masks):
    slots, half = own.shape
    block = 2 * half // replicas
    return pl.pallas_call(
        functools.partial(merge_kernel, experts, shard_rows, masks, replicas // 8),
        out_shape=[jax.ShapeDtypeStruct((2, 2, slots, block), bf16)] * len(masks),
        in_specs=[smem()] + [vmem()] * (experts + 1),
        out_specs=[vmem()] * len(masks),
        scratch_shapes=[pltpu.VMEM((replicas // 2, slots, block), bf16)],
        compiler_params=params(own, own, own, *incoming),
        cost_estimate=LIGHT,
        name="merged_rows",
    )(where, index, own, *incoming)


def forward_kernel(uppers, blocks, where_ref, *refs):
    own, crossed_ref, rest, outs = refs[:uppers], refs[uppers], refs[uppers + 1 :], refs[uppers + 1 + len(blocks.arrays) :]
    side = where_ref[4]
    totals = [jnp.zeros(outs[0].shape, f32) for _ in range(4)]
    for mask in range(uppers):
        peer = crossed_ref.at[mask]
        for side_mask in range(2):
            w = blocks.ref(rest, 4 * mask + 2 * side_mask)
            for rows, first in ((own[mask].at[0], 0), (peer, 2)):
                for matrix in range(2):
                    totals[first + matrix] += jnp.dot(rows[side ^ side_mask], w[matrix], preferred_element_type=f32)
    for out, total in zip(outs, totals):
        out[...] = total


def forward(where, crossed, own, blocks, uppers):
    out = jax.ShapeDtypeStruct((own[0].shape[2], blocks.arrays[0].shape[-1]), f32)
    return pl.pallas_call(
        functools.partial(forward_kernel, uppers, blocks),
        out_shape=[out] * 4,
        in_specs=[smem()] + [vmem()] * (uppers + 1 + len(blocks.arrays)),
        out_specs=[vmem()] * 4,
        compiler_params=params(*own, crossed, *blocks.arrays),
        cost_estimate=LIGHT,
        name="forward_values",
    )(where, *own, crossed, *blocks.arrays)


def delta_kernel(where_ref, count_ref, targets_ref, gate_ref, up_ref, gate_other_ref, up_other_ref, kept_ref, sent_ref):
    side = where_ref[4]
    slots = targets_ref.shape[0]
    gate_value = gate_ref[...] + gate_other_ref[...]
    up_value = up_ref[...] + up_other_ref[...]
    live_count = count_ref[0, 0]
    sigmoid = jax.nn.sigmoid(gate_value)
    activated = gate_value * sigmoid
    silu_slope = sigmoid * (1.0 + gate_value * (1.0 - sigmoid))
    live = (grid_iota((slots, 1), 0) < live_count).astype(f32)
    residual = (activated * up_value - targets_ref[...].astype(f32)) * live / jnp.full((1, 1), live_count, i32).astype(f32)
    gate_delta = (residual * up_value * silu_slope).astype(bf16)
    up_delta = (residual * activated).astype(bf16)
    kept_ref[...] = jnp.where(side == 0, gate_delta, up_delta)
    sent_ref[...] = jnp.where(side == 0, up_delta, gate_delta)


def deltas_of(where, count, targets, values):
    out = jax.ShapeDtypeStruct(targets.shape, bf16)
    return pl.pallas_call(
        delta_kernel,
        out_shape=[out, out],
        in_specs=[smem(), smem()] + [vmem()] * (1 + len(values)),
        out_specs=[vmem()] * 2,
        compiler_params=params(targets, *values),
        cost_estimate=LIGHT,
        name="deltas",
    )(where, count, targets, *values)


def token_contract(left, right):
    return lax.dot_general(left, right, (((0,), (0,)), ((), ())), preferred_element_type=f32)


TILE = 16


class Pieces:
    def __init__(self):
        self.arrays, self.place = [], {}

    def put(self, keys, pieces):
        if isinstance(pieces, list):
            for key, piece in zip(keys, pieces):
                self.place[key] = (len(self.arrays), None)
                self.arrays.append(piece)
            return
        for index, key in enumerate(keys):
            self.place[key] = (len(self.arrays), index)
        self.arrays.append(pieces)

    def ref(self, refs, key):
        array, index = self.place[key]
        return refs[array] if index is None else refs[array].at[index]

    def read(self, refs, key):
        return self.ref(refs, key)[...]


def split_refs(rows, deltas, refs):
    count = len(rows.arrays)
    rest = refs[count:]

    def rows_of(key):
        ref = rows.ref(refs, key)
        return ref.at[0] if len(ref.shape) == 4 else ref

    return rows_of, lambda key: deltas.read(rest, key), rest[len(deltas.arrays) :]


def gram_kernel(replicas, pieces, where_ref, *refs):
    rows, deltas, (gram_ref, table_ref) = split_refs(*pieces, refs)
    me = where_ref[5]
    block = rows(0).shape[2]
    steps = block // TILE
    for mask in range(replicas):
        first = pl.multiple_of((me ^ mask) * TILE, TILE)
        for part in range(2):
            gradient = token_contract(rows(mask)[part], deltas(mask)).astype(bf16)
            for step in range(steps):
                table_ref[part * steps + step, pl.ds(first, TILE), :] = gradient[step * TILE : (step + 1) * TILE]
    size = replicas * TILE
    products = jnp.zeros((size, size), f32)
    for step in range(2 * steps):
        products += lax.dot_general(
            table_ref[step], table_ref[step], (((1,), (1,)), ((), ())), preferred_element_type=f32
        )
    same = (grid_iota((size, size), 0) & (TILE - 1)) == (grid_iota((size, size), 1) & (TILE - 1))
    products = jnp.where(same, products, 0.0)
    down = jnp.concatenate(
        [jnp.sum(products[r * TILE : (r + 1) * TILE], axis=0, keepdims=True) for r in range(replicas)], axis=0
    )
    member = (grid_iota((size, replicas), 0) // TILE == grid_iota((size, replicas), 1)).astype(f32)
    gram_ref[...] = jnp.dot(down, member, preferred_element_type=f32, precision=lax.Precision.HIGHEST)


def gram(where, rows, deltas, replicas):
    depth = 2 * rows.arrays[0].shape[-1]
    hidden = deltas.arrays[0].shape[-1]
    return pl.pallas_call(
        functools.partial(gram_kernel, replicas, (rows, deltas)),
        out_shape=jax.ShapeDtypeStruct((replicas, replicas), f32),
        in_specs=[smem()] + [vmem()] * (len(rows.arrays) + len(deltas.arrays)),
        out_specs=vmem(),
        scratch_shapes=[pltpu.VMEM((depth // TILE, replicas * TILE, hidden), bf16)],
        compiler_params=params(*rows.arrays, *deltas.arrays, jax.ShapeDtypeStruct((replicas * TILE, replicas * TILE), f32)),
        cost_estimate=LIGHT,
        name="gradient_products",
    )(where, *rows.arrays, *deltas.arrays)


def tree_weights(table, replicas):
    down, along = grid_iota((replicas, replicas), 0), grid_iota((replicas, replicas), 1)
    weights = jnp.ones((replicas, 1), f32)
    half = replicas // 2
    while half >= 1:
        same = down == along
        other = ((down + half) & (replicas - 1)) == along
        partner = ((along + half) & (replicas - 1)) == down
        square_down = jnp.sum(jnp.where(same, table, 0.0), axis=1, keepdims=True)
        square_along = jnp.sum(jnp.where(same, table, 0.0), axis=0, keepdims=True)
        inner_down = jnp.sum(jnp.where(other, table, 0.0), axis=1, keepdims=True)
        inner_along = jnp.sum(jnp.where(partner, table, 0.0), axis=0, keepdims=True)
        weight_down = 1.0 - inner_down / (2.0 * square_down + adasum_epsilon)
        weight_along = 1.0 - inner_along / (2.0 * square_along + adasum_epsilon)
        weights = weights * weight_down
        table = weight_down * (table * weight_along)
        table = table + jnp.concatenate([table[half:], table[:half]], axis=0)
        table = table + jnp.concatenate([table[:, half:], table[:, :half]], axis=1)
        half //= 2
    return weights


def combine_kernel(replicas, pieces, sent, where_ref, gram_ref, *refs):
    rows, deltas, (out_ref, weight_ref) = split_refs(*pieces, refs)
    side, me = where_ref[4], where_ref[5]
    weight_ref[...] = jnp.broadcast_to(tree_weights(gram_ref[...], replicas), weight_ref.shape)
    part = 1 - side if sent else side
    total = jnp.zeros(out_ref.shape, f32)
    for mask in range(replicas):
        gradient = token_contract(rows(mask)[part], deltas(mask))
        total = total + weight_ref[pl.ds(me ^ mask, 1), 0:1] * gradient
    out_ref[...] = total


def combine(where, products, rows, deltas, sent):
    replicas = products.shape[0]
    out = jax.ShapeDtypeStruct((rows.arrays[0].shape[-1], deltas.arrays[0].shape[-1]), f32)
    return pl.pallas_call(
        functools.partial(combine_kernel, replicas, (rows, deltas), sent),
        out_shape=out,
        in_specs=[smem(), vmem()] + [vmem()] * (len(rows.arrays) + len(deltas.arrays)),
        out_specs=vmem(),
        scratch_shapes=[pltpu.VMEM((replicas, 128), f32)],
        compiler_params=params(*rows.arrays, *deltas.arrays),
        cost_estimate=LIGHT,
        name="combined_gradient",
    )(where, products, *rows.arrays, *deltas.arrays)


def shards(pool, row_index, counts, targets, weights, first_moment, second_moment):
    replicas = lax.axis_size("replica")
    experts = lax.axis_size("expert")
    uppers = replicas // 4
    position = lax.axis_index("replica")
    expert_position = lax.axis_index("expert")
    core, side, upper = position & 1, position >> 1 & 1, position >> 2
    where = jnp.stack([expert_position, position // (replicas // 2), upper, core, side, position]).astype(i32)
    index = row_index[:, 0, :]
    local_pool = pool[0]
    shard_rows = local_pool.shape[0]
    most = 3 * index.shape[1] // (2 * experts)

    halves = uppers // 2
    upper_masks = [4 << bit for bit in range(uppers.bit_length() - 1)]
    picks = picks_of(where, index, experts, most, shard_rows)
    far, near = list(range(halves, uppers)), list(range(halves))
    packed = [None] * uppers
    for part, masks in enumerate((far, near)):
        outgoing, own = listed_rows(where, picks, local_pool, experts, most, part)
        incoming = [swapped(outgoing[mask - 1 : mask], "expert", mask) for mask in range(1, experts)]
        if part == 0:
            lowered = weights[0].astype(bf16)
            by_upper = gathered(lowered, upper_masks)
            by_upper = [by_upper[4 * mask] for mask in range(uppers)]
            own, picks, *_ = lax.optimization_barrier((own, picks, by_upper[halves], by_upper[1]))
            blocks = Pieces()
            blocks.put([4 * mask for mask in range(uppers)], by_upper)
            besides = []
            for group in (near, far):
                besides.append(swapped(jnp.stack([by_upper[mask] for mask in group]), "replica", SIDE))
                blocks.put([4 * mask | SIDE for mask in group], besides[-1])
        else:
            own, _ = lax.optimization_barrier((own, besides[0]))
        packed[masks[0] : masks[-1] + 1] = merged_rows(
            where, index, own, incoming, experts, replicas, shard_rows, masks
        )

    crossed = swapped(jnp.stack([piece[1] for piece in packed]), "replica", CORE)
    values = forward(where, crossed, packed, blocks, uppers)

    rows = Pieces()
    rows.put([0], [packed[0]])
    others_of = far + near[1:]
    arrived = [swapped(packed[mask], "replica", 4 * mask) for mask in others_of]
    other = swapped(jnp.stack([piece[1] for piece in arrived]), "replica", CORE)
    for mask, piece in zip(others_of, arrived):
        rows.put([4 * mask], [piece])
    rows.put([4 * mask | CORE for mask in others_of], other)
    rows.put([CORE], crossed)
    values = list(values[:2]) + [swapped(value, "replica", CORE) for value in values[2:]]
    kept_delta, sent_delta = deltas_of(where, counts, targets[0, 0], values)
    side_deltas = [kept_delta, swapped(sent_delta, "replica", SIDE)]

    deltas = Pieces()
    far_mask, near_masks = upper_masks[-1], upper_masks[:-1]

    def hold(keys, pieces):
        both = jnp.stack(pieces)
        deltas.put(keys, both)
        across = swapped(both, "replica", CORE)
        deltas.put([key | CORE for key in keys], across)
        return both, across

    hold([0, SIDE], side_deltas)
    kept_far = swapped(kept_delta, "replica", far_mask)
    kept_near, beside_near = [gathered(piece, near_masks) for piece in side_deltas]
    keys = [mask for mask in kept_near if mask > 0]
    kept_near, beside_near = [kept_near[key] for key in keys], [beside_near[key] for key in keys]
    beside_own, *_ = lax.optimization_barrier((side_deltas[1], *kept_near))
    beside_far = swapped(beside_own, "replica", far_mask)
    all_here = [packed[0][0]] + [piece[0] for piece in arrived] + [crossed[0]] + [other[i] for i in range(len(arrived))]
    all_here, _ = lax.optimization_barrier((jnp.stack(all_here), side_deltas[1]))
    keys_beside = [4 * mask | SIDE for mask in [0] + others_of]
    rows.put(keys_beside + [key | CORE for key in keys_beside], swapped(all_here, "replica", SIDE))
    hold(keys + [key | SIDE for key in keys], kept_near + beside_near)
    far, _ = hold([far_mask, far_mask | SIDE], [kept_far, beside_far])
    far, *_ = lax.optimization_barrier((far, *kept_near, *beside_near))
    for key, piece in gathered(far, near_masks).items():
        if key > 0:
            keys = [far_mask | key, far_mask | key | SIDE]
            deltas.put(keys, piece)
            deltas.put([key | CORE for key in keys], swapped(piece, "replica", CORE))

    products = gram(where, rows, deltas, replicas)
    products = products + swapped(products, "replica", CORE)
    mask = 4
    while mask < replicas:
        products = products + swapped(products, "replica", mask)
        mask *= 2
    sent_block = combine(where, products, rows, deltas, True)
    other_block = swapped(sent_block, "replica", SIDE)
    kept_block = combine(where, products, rows, deltas, False)
    combined = jnp.where(
        side == 0, jnp.stack([kept_block, other_block]), jnp.stack([other_block, kept_block])
    )
    new_weight, moment_one, moment_two = adam_update(
        combined, weights[0], first_moment[0], second_moment[0]
    )
    return (new_weight[None], moment_one[None], moment_two[None])


def solution(mesh):
    in_specs = (
        P("replica", "expert", None),
        P(None, "replica", None),
        P("expert", "replica"),
        P("expert", "replica", None, None),
        P("expert", None, "replica", None),
        P("expert", None, "replica", None),
        P("expert", None, "replica", None),
    )
    out_specs = (
        P("expert", None, "replica", None),
        P("expert", None, "replica", None),
        P("expert", None, "replica", None),
    )
    return jax.shard_map(shards, mesh=mesh, in_specs=in_specs, out_specs=out_specs, check_vma=False)
```
